32 devices in a mesh: dp: 4 (over z), proto: 8 (over y, x, core).
Axes of the slice: x: 2, y: 2, z: 4, core: 2. Of those that a mesh axis runs over, the one named last changes fastest.
Arguments:
- embeddings: bfloat16 [8192, 2560], P('proto', 'dp'), may hold values from -26 to 26
- table: bfloat16 [32768, 2560], P('proto', 'dp'), may hold values from -5 to 5
- tile_lists: int32 [8, 8], replicated, may hold values from 0 to 255, as said below
- labels: int32 [8192], P('proto'), may hold values from 0 to 32767, as said below
Outputs:
- loss: float32 [], replicated
- grad_emb: bfloat16 [8192, 2560], P('proto', 'dp')
- grad_table: bfloat16 [32768, 2560], P('proto', 'dp')
The draws below stay inside these ranges and needn't reach their ends.
Inputs may be any that keep to these rules, and one draw needn't show every extreme that they name: `tile_lists`: each block's 8 tile ids are distinct and fall on exactly 4 owners (owner = id // 32), each of those owners holding exactly 2 of them. `labels`: the tile of each row's label (label // 128) is in the list of the row's block.
All inputs are finite; a program needn't handle non-finite values.
Results may differ from the reference program's by a relative error of at most 0.0025.
The reference program's roundings to bfloat16 on the way count: a program that leaves them out, or rounds other values in their place, can miss the bound.
Values may be sent and summed in bfloat16 or wider, within the bound.
A program may use at most 128 MiB of HBM per device.

```python
import math
import jax
import jax.numpy as jnp
from jax import lax

D = 2560
TILE = 128
CAP = 2
TILES_DEV = 32
K = 8
BLOCK = 1024
BLOCKS = 8
ROWS = 8192
NPROTO = 32768


def make_lists(key):
    base = jax.random.fold_in(key, 101)
    keys = jax.random.split(base, BLOCKS)

    def one_block(block_key):
        first_key, second_key = jax.random.split(block_key)
        owners = jax.random.permutation(first_key, BLOCKS)[:K // CAP]
        picks = jax.vmap(lambda inner: jax.random.permutation(inner, TILES_DEV)[:CAP])(jax.random.split(second_key, K // CAP))
        return (owners[:, None] * TILES_DEV + picks).reshape(K).astype(jnp.int32)
    return jax.vmap(one_block)(keys)


def make_labels(key):
    lists = make_lists(key)
    first_key, second_key = jax.random.split(jax.random.fold_in(key, 202))
    slot = jax.random.randint(first_key, (BLOCKS, BLOCK), 0, K)
    offset = jax.random.randint(second_key, (BLOCKS, BLOCK), 0, TILE)
    chosen = jnp.take_along_axis(lists, slot, axis=1)
    return (chosen * TILE + offset).reshape(ROWS).astype(jnp.int32)


def table_rows(key, index):
    base = jax.random.fold_in(key, 303)

    def one_row(row):
        row_key = jax.random.fold_in(base, row)
        return jnp.clip(jax.random.normal(row_key, (D,), jnp.float32), -5.0, 5.0)
    return jax.vmap(one_row)(index)


def draw_tile_lists(key, part):
    return make_lists(key)


def draw_labels(key, part):
    return make_labels(key)


def draw_table(key, part):
    return table_rows(key, jnp.arange(NPROTO, dtype=jnp.int32)).astype(jnp.bfloat16)


def draw_embeddings(key, part):
    base = jax.random.fold_in(key, 404)
    return jnp.clip(jax.random.normal(base, (ROWS, D), jnp.float32), -5.0, 5.0).astype(jnp.bfloat16)


def setup_inputs(seed: int = 0) -> dict:
    key_of = jax.random.split(jax.random.key(seed), 5)
    return {
        "embeddings": draw_embeddings(jax.random.fold_in(key_of[4], 71), 0),
        "table": draw_table(jax.random.fold_in(key_of[4], 71), 0),
        "tile_lists": draw_tile_lists(jax.random.fold_in(key_of[4], 71), 0),
        "labels": draw_labels(jax.random.fold_in(key_of[4], 71), 0),
    }


def block_terms(emb_block, table, ids, lab):
    tiles = jnp.take(table.reshape(TILES_DEV * BLOCKS, TILE, D), ids, axis=0).reshape(K * TILE, D)
    scores = lax.dot_general(emb_block, tiles, (((1,), (1,)), ((), ())), preferred_element_type=jnp.float32) / math.sqrt(D)
    hit = (ids[None, :] == (lab // TILE)[:, None]).astype(jnp.int32)
    column = lax.optimization_barrier(jnp.sum(hit * (jnp.arange(K, dtype=jnp.int32) * TILE)[None, :], axis=1)) + lab % TILE
    onehot = (jnp.arange(K * TILE, dtype=jnp.int32)[None, :] == column[:, None]).astype(jnp.float32)
    top = lax.optimization_barrier(jnp.max(scores, axis=1, keepdims=True))
    expo = jnp.exp(scores - top)
    total = lax.optimization_barrier(jnp.sum(expo, axis=1, keepdims=True))
    lse = top[:, 0] + jnp.log(total[:, 0])
    target = lax.optimization_barrier(jnp.sum(scores * onehot, axis=1))
    loss_sum = jnp.sum(lse - target)
    dz_block = (expo / total - onehot).astype(jnp.bfloat16)
    grad_rows = jnp.dot(dz_block, tiles, preferred_element_type=jnp.float32).astype(jnp.bfloat16)
    piece = lax.dot_general(dz_block, emb_block, (((0,), (0,)), ((), ())), preferred_element_type=jnp.float32).astype(jnp.bfloat16)
    return (loss_sum, grad_rows, piece)

def reference(embeddings, table, tile_lists, labels):
    emb_blocks = embeddings.reshape(BLOCKS, BLOCK, D)
    lab_blocks = labels.reshape(BLOCKS, BLOCK)

    def step(carry, inputs):
        accum, loss_acc = carry
        emb_block, ids, lab = inputs
        loss_sum, grad_rows, piece = block_terms(emb_block, table, ids, lab)
        accum = accum.at[ids].add(piece.reshape(K, TILE, D).astype(jnp.float32))
        return ((accum, loss_acc + loss_sum), grad_rows)
    start = (jnp.zeros((TILES_DEV * BLOCKS, TILE, D), jnp.float32), jnp.zeros((), jnp.float32))
    (accum, loss_acc), grads = lax.scan(step, start, (emb_blocks, tile_lists, lab_blocks))
    loss = loss_acc / ROWS
    grad_emb = grads.reshape(ROWS, D)
    grad_table = accum.reshape(NPROTO, D).astype(jnp.bfloat16)
    return (loss, grad_emb, grad_table)
```

```python
import functools
import math

import jax
import jax.numpy as jnp
from jax import lax
from jax.experimental import pallas as pl
from jax.experimental.pallas import tpu as pltpu
from jax.sharding import PartitionSpec as P

D = 2560
TILE = 128
CAP = 2
PARTS = 4
CHUNK = {False: 32, True: 64}
DZ_CHUNK = 64
LAG = 4
DZ_LAG = 4
CODED = False
CODE_MAX = 32766.0
ROUND = 12582912.0
VMEM_LIMIT = 56 * 2**20
MESH = pl.DeviceIdType.MESH


def slot_plan(ids, tiles_here):
    owners = ids // tiles_here
    local = ids % tiles_here
    count = ids.shape[-1]
    before = jnp.arange(count)[:, None] > jnp.arange(count)[None, :]
    earlier = (owners[..., :, None] == owners[..., None, :]) & before
    rank = jnp.sum(earlier.astype(jnp.int32), axis=-1)
    return (owners, local, rank)


def softmax_terms(scores, ids, lab, list_len):
    hit = (ids[None, :] == (lab // TILE)[:, None]).astype(jnp.int32)
    column = (
        jnp.sum(hit * (jnp.arange(list_len, dtype=jnp.int32) * TILE)[None, :], axis=1) + lab % TILE
    )
    onehot = (jnp.arange(list_len * TILE, dtype=jnp.int32)[None, :] == column[:, None]).astype(
        jnp.float32
    )
    top = jnp.max(scores, axis=1, keepdims=True)
    expo = jnp.exp(scores - top)
    total = jnp.sum(expo, axis=1, keepdims=True)
    lse = top[:, 0] + jnp.log(total[:, 0])
    target = jnp.sum(scores * onehot, axis=1)
    dz_rows = (expo / total - onehot).astype(jnp.bfloat16)
    return (jnp.sum(lse - target), dz_rows)


def body(embeddings, table, tile_lists, labels):
    block_rows, width = embeddings.shape
    list_len = tile_lists.shape[1]
    tiles_here = table.shape[0] // TILE
    groups = lax.axis_size("proto")
    dp_count = lax.axis_size("dp")
    rows_dev = block_rows // dp_count
    total_rows = block_rows * groups
    me = lax.axis_index("proto")
    part = lax.axis_index("dp")
    inv_scale = 1.0 / math.sqrt(D)
    owners, local, rank = slot_plan(tile_lists, tiles_here)
    match = (owners == me)[:, :, None] & (
        rank[:, :, None] == jnp.arange(CAP, dtype=jnp.int32)[None, None, :]
    )
    select = jnp.sum(match.astype(jnp.int32) * local[:, :, None], axis=1)
    shaped_table = table.reshape(tiles_here, TILE, width)
    outgoing = pack_tiles(shaped_table, select.reshape(-1)).reshape(groups, CAP, TILE, width)
    incoming = lax.all_to_all(outgoing, "proto", split_axis=0, concat_axis=0, tiled=True)
    my_ids = lax.dynamic_index_in_dim(tile_lists, me, 0, keepdims=False)
    my_owner = lax.dynamic_index_in_dim(owners, me, 0, keepdims=False)
    my_rank = lax.dynamic_index_in_dim(rank, me, 0, keepdims=False)
    flat_slot = my_owner * CAP + my_rank
    tiles = pack_tiles(incoming.reshape(groups * CAP, TILE, width), flat_slot).reshape(
        list_len * TILE, width
    )
    scores = (
        lax.psum_scatter(
            lax.dot_general(
                embeddings, tiles, (((1,), (1,)), ((), ())), preferred_element_type=jnp.float32
            ),
            "dp",
            scatter_dimension=0,
            tiled=True,
        )
        * inv_scale
    )
    my_labels = lax.dynamic_slice_in_dim(labels, part * rows_dev, rows_dev, 0)
    loss_part, dz_rows = softmax_terms(scores, my_ids, my_labels, list_len)
    dz_block = lax.all_gather(dz_rows, "dp", axis=0, tiled=True)
    loss = lax.psum(loss_part, ("dp", "proto")) / total_rows
    grad_emb = jnp.dot(dz_block, tiles, preferred_element_type=jnp.float32).astype(jnp.bfloat16)
    piece = lax.dot_general(
        dz_block, embeddings, (((0,), (0,)), ((), ())), preferred_element_type=jnp.float32
    ).astype(jnp.bfloat16)
    returning = (
        jnp.zeros((groups * CAP, TILE, width), jnp.bfloat16)
        .at[flat_slot]
        .set(piece.reshape(list_len, TILE, width))
    )
    returned = lax.all_to_all(
        returning.reshape(groups, CAP, TILE, width),
        "proto",
        split_axis=0,
        concat_axis=0,
        tiled=True,
    )
    accum = (
        jnp.zeros((tiles_here, TILE, width), jnp.float32)
        .at[select.reshape(-1)]
        .add(returned.reshape(groups * CAP, TILE, width))
    )
    grad_table = accum.reshape(tiles_here * TILE, width).astype(jnp.bfloat16)
    return (loss, grad_emb, grad_table)


def pack_kernel(pick_ref, table_ref, out_ref, sems):
    count = out_ref.shape[0]

    def copy(slot):
        return pltpu.make_async_copy(
            table_ref.at[pick_ref[slot]], out_ref.at[slot], sems.at[slot]
        )

    for slot in range(count):
        copy(slot).start()
    for slot in range(count):
        copy(slot).wait()


def pack_tiles(shaped_table, pick):
    count = pick.shape[0]
    _, tile, width = shaped_table.shape
    return pl.pallas_call(
        pack_kernel,
        out_shape=jax.ShapeDtypeStruct((count, tile, width), shaped_table.dtype),
        grid_spec=pltpu.PrefetchScalarGridSpec(
            num_scalar_prefetch=1,
            grid=(1,),
            in_specs=[pl.BlockSpec(memory_space=pl.ANY)],
            out_specs=pl.BlockSpec(memory_space=pltpu.VMEM),
            scratch_shapes=[pltpu.SemaphoreType.DMA((count,))],
        ),
        compiler_params=pltpu.CompilerParams(vmem_limit_bytes=32 * 2**20),
    )(pick, shaped_table)


def place_kernel(lists, returned, emb_in, loss_in, table_out, emb_out, loss_out, got, emb, zero, sums, count, first, second, slots, in_sem, emb_sem, out_sem):
    me = lax.axis_index("proto")
    blocks, list_len = lists.shape
    tiles_here = table_out.shape[0]
    load = pltpu.make_async_copy(returned, got, in_sem)
    load.start()
    load_emb = pltpu.make_async_copy(emb_in, emb, emb_sem)
    load_emb.start()
    zero[...] = jnp.zeros_like(zero)
    base = me * tiles_here

    def clear(t, carry):
        count[t] = 0
        first[t] = 0
        return carry

    lax.fori_loop(0, tiles_here, clear, 0)

    def note(b, carry):
        slots[0] = b * CAP
        for j in range(list_len):
            tile = lists[b, j] - base

            @pl.when((tile >= 0) & (tile < tiles_here))
            def _():
                seen = count[tile]
                second[tile] = first[tile]
                first[tile] = slots[0]
                count[tile] = seen + 1
                slots[0] = slots[0] + 1

        return carry

    lax.fori_loop(0, blocks, note, 0)

    def from_zero(t):
        return pltpu.make_async_copy(zero, table_out.at[t], out_sem.at[t])

    def zeros(t, carry):
        @pl.when(count[t] == 0)
        def _():
            from_zero(t).start()

        return carry

    lax.fori_loop(0, tiles_here, zeros, 0)
    loss_out[0, 0] = jnp.max(loss_in[0:1, :])
    load_emb.wait()
    save_emb = pltpu.make_async_copy(emb, emb_out, emb_sem)
    save_emb.start()
    load.wait()

    def ones(t, carry):
        @pl.when(count[t] == 1)
        def _():
            pltpu.make_async_copy(got.at[first[t]], table_out.at[t], out_sem.at[t]).start()

        return carry

    lax.fori_loop(0, tiles_here, ones, 0)

    def many(t, carry):
        @pl.when(count[t] == 2)
        def _():
            total = got[first[t]].astype(jnp.float32) + got[second[t]].astype(jnp.float32)
            got[first[t]] = total.astype(got.dtype)
            pltpu.make_async_copy(got.at[first[t]], table_out.at[t], out_sem.at[t]).start()

        @pl.when(count[t] > 2)
        def _():
            sums[...] = jnp.zeros_like(sums)

            def block(b, carry):
                slots[0] = b * CAP
                for j in range(list_len):
                    tile = lists[b, j] - base

                    @pl.when((tile >= 0) & (tile < tiles_here))
                    def _():
                        @pl.when(tile == t)
                        def _():
                            sums[...] += got[slots[0]].astype(jnp.float32)

                        slots[0] = slots[0] + 1

                return carry

            lax.fori_loop(0, blocks, block, 0)
            got[first[t]] = sums[...].astype(got.dtype)
            pltpu.make_async_copy(got.at[first[t]], table_out.at[t], out_sem.at[t]).start()

        return carry

    lax.fori_loop(0, tiles_here, many, 0)

    def drain(t, carry):
        from_zero(t).wait()
        return carry

    lax.fori_loop(0, tiles_here, drain, 0)
    save_emb.wait()


def place_tiles(lists, returned, grad_emb, loss, tiles_here):
    count, tile, width = returned.shape
    smem = pl.BlockSpec(memory_space=pltpu.SMEM)
    vmem = pl.BlockSpec(memory_space=pltpu.VMEM)
    hbm = pl.BlockSpec(memory_space=pltpu.HBM)
    dma = pltpu.SemaphoreType.DMA
    return pl.pallas_call(
        place_kernel,
        out_shape=(
            jax.ShapeDtypeStruct((tiles_here, tile, width), returned.dtype),
            jax.ShapeDtypeStruct(grad_emb.shape, grad_emb.dtype),
            jax.ShapeDtypeStruct((1, 1), jnp.float32),
        ),
        in_specs=[smem, hbm, hbm, vmem],
        out_specs=(hbm, hbm, smem),
        scratch_shapes=[
            pltpu.VMEM(returned.shape, returned.dtype),
            pltpu.VMEM(grad_emb.shape, grad_emb.dtype),
            pltpu.VMEM((tile, width), returned.dtype),
            pltpu.VMEM((tile, width), jnp.float32),
            pltpu.SMEM((tiles_here,), jnp.int32),
            pltpu.SMEM((tiles_here,), jnp.int32),
            pltpu.SMEM((tiles_here,), jnp.int32),
            pltpu.SMEM((1,), jnp.int32),
            dma,
            dma,
            dma((tiles_here,)),
        ],
        compiler_params=pltpu.CompilerParams(vmem_limit_bytes=VMEM_LIMIT),
    )(lists, returned, grad_emb, loss)


def main_kernel(
    coded,
    groups,
    dp_count,
    tiles_here,
    lists,
    labels,
    emb_hbm,
    table_hbm,
    grad_hbm,
    returned,
    loss_out,
    table,
    emb,
    out_tiles,
    tiles,
    scores,
    partial,
    outgo,
    bound_in,
    bound_out,
    bound_top,
    column,
    dz,
    piece,
    ret,
    grad,
    loss_acc,
    loss_mine,
    loss_plane,
    loss_sum,
    loss_z,
    select,
    my_slot,
    back,
    table_sem,
    emb_sem,
    grad_sem,
    tile_send,
    tile_recv,
    part_send,
    part_recv,
    bound_send,
    bound_recv,
    dz_send,
    dz_recv,
    ret_send,
    ret_recv,
    own_ret_sem,
    lp_send,
    lp_recv,
    lz_send,
    lz_recv,
    *incoming,
):
    me = lax.axis_index("proto")
    z = lax.axis_index("dp")
    rows, width = emb.shape
    list_len = lists.shape[1]
    parts, cols, _ = tiles.shape
    piece_rows = TILE // parts
    chunk = CHUNK[coded]
    half = rows // 2
    chunks = half // chunk
    dz_chunks = half // DZ_CHUNK
    ratio = DZ_CHUNK // chunk
    last = dp_count - 1
    inv_scale = 1.0 / math.sqrt(D)

    barrier = pltpu.get_barrier_semaphore()
    for k in range(1, groups):
        pl.semaphore_signal(
            barrier, inc=1, device_id={"proto": lax.rem(me + k, groups)}, device_id_type=MESH
        )
    for k in range(1, dp_count):
        pl.semaphore_signal(
            barrier, inc=1, device_id={"dp": lax.rem(z + k, dp_count)}, device_id_type=MESH
        )
    load_table = pltpu.make_async_copy(table_hbm, table, table_sem)
    load_table.start()
    load_emb = pltpu.make_async_copy(emb_hbm, emb, emb_sem)
    load_emb.start()

    base = me * tiles_here
    for b in range(groups):
        local = [lists[b, j] - base for j in range(list_len)]
        mine = [(t >= 0) & (t < tiles_here) for t in local]
        low, high = jnp.int32(0), jnp.int32(0)
        for j in range(list_len):
            high = jnp.where(mine[j], local[j], high)
            back_j = list_len - 1 - j
            low = jnp.where(mine[back_j], local[back_j], low)
        select[b * CAP] = low
        select[b * CAP + 1] = high

    load_table.wait()
    for k in range(groups):
        to = lax.rem(me + k, groups)
        for t in range(CAP):
            slot = to * CAP + t
            for g in range(parts):
                block = table[select[slot], g * piece_rows : (g + 1) * piece_rows, :]
                if k == 0:
                    incoming[g][slot] = block
                else:
                    out_tiles[g, slot] = block
    pl.semaphore_wait(barrier, groups + dp_count - 2)

    def tile_copy(g, k):
        to = lax.rem(me + k, groups)
        return pltpu.make_async_remote_copy(
            src_ref=out_tiles.at[g, pl.ds(to * CAP, CAP)],
            dst_ref=incoming[g].at[pl.ds(me * CAP, CAP)],
            send_sem=tile_send.at[g, k],
            recv_sem=tile_recv.at[g, k],
            device_id={"proto": to},
            device_id_type=MESH,
        )

    for g in range(parts):
        for k in range(1, groups):
            tile_copy(g, k).start()

    ids = [lists[me, j] for j in range(list_len)]
    owner = [lax.div(t, jnp.int32(tiles_here)) for t in ids]
    flat = []
    for j in range(list_len):
        rank = jnp.int32(0)
        for i in range(j):
            rank = rank + jnp.where(owner[i] == owner[j], 1, 0)
        flat.append(owner[j] * CAP + rank)
        my_slot[j] = flat[j]
    for s in range(groups * CAP):
        at = jnp.int32(0)
        for j in range(1, list_len):
            at = jnp.where(flat[j] == s, j, at)
        back[s] = at
    lab = labels[...]
    lab_tile = lax.shift_right_logical(lab, 7)
    within = lax.bitwise_and(lab, TILE - 1)
    part_of = lax.shift_right_logical(within, int(math.log2(piece_rows)))
    where_to = part_of * cols + lax.bitwise_and(within, piece_rows - 1)
    for j in range(list_len):
        where_to = where_to + jnp.where(lab_tile == ids[j], j * piece_rows, 0)
    for i in range(rows // 128):
        column[i * 128 : (i + 1) * 128, :] = jnp.broadcast_to(where_to[i : i + 1, :], (128, 128)).T

    loss_acc[...] = jnp.zeros_like(loss_acc)
    bound_top[...] = jnp.zeros_like(bound_top)
    load_emb.wait()

    def tiles_in(g):
        for k in range(1, groups):
            tile_copy(g, k).wait()
        for j in range(list_len):
            tiles[g, j * piece_rows : (j + 1) * piece_rows, :] = incoming[g][my_slot[j]]

    def rows_of(way, at):
        return pl.multiple_of((1 - way) * half + at, 32)

    def part_copy(way, g, c, first):
        here = pl.ds(pl.multiple_of(c * chunk, chunk), chunk)
        dst = partial.at[way, g, here]
        if coded:
            src = outgo.at[way, g, here]
        elif first:
            src = scores.at[g, pl.ds(rows_of(way, c * chunk), chunk)]
        else:
            src = dst
        return pltpu.make_async_remote_copy(
            src_ref=src,
            dst_ref=dst,
            send_sem=part_send.at[way, g, c],
            recv_sem=part_recv.at[way, g, c],
            device_id={"dp": jnp.clip(z + 1 - 2 * way, 0, last)},
            device_id_type=MESH,
        )

    def bound_copy(way, g):
        return pltpu.make_async_remote_copy(
            src_ref=bound_out.at[way, g],
            dst_ref=bound_in.at[way, g],
            send_sem=bound_send.at[way, g],
            recv_sem=bound_recv.at[way, g],
            device_id={"dp": jnp.clip(z + 1 - 2 * way, 0, last)},
            device_id_type=MESH,
        )

    def dz_copy(way, u):
        at = dz.at[u // dz_chunks, pl.ds(rows_of(way, lax.rem(u, dz_chunks) * DZ_CHUNK), DZ_CHUNK)]
        return pltpu.make_async_remote_copy(
            src_ref=at,
            dst_ref=at,
            send_sem=dz_send.at[way, u],
            recv_sem=dz_recv.at[way, u],
            device_id={"dp": jnp.clip(z - 1 + 2 * way, 0, last)},
            device_id_type=MESH,
        )

    def ret_copy(q, k):
        to = lax.rem(me + k, groups)
        return pltpu.make_async_remote_copy(
            src_ref=ret.at[q, pl.ds(to * CAP, CAP)],
            dst_ref=returned.at[pl.ds(me * CAP, CAP), pl.ds(pl.multiple_of(q * piece_rows, 16), piece_rows)],
            send_sem=ret_send.at[q, k],
            recv_sem=ret_recv.at[q, k],
            device_id={"proto": to},
            device_id_type=MESH,
        )

    def own_ret(q):
        return pltpu.make_async_copy(
            ret.at[q, pl.ds(me * CAP, CAP)],
            returned.at[pl.ds(me * CAP, CAP), pl.ds(pl.multiple_of(q * piece_rows, 16), piece_rows)],
            own_ret_sem.at[q],
        )

    lane = lax.broadcasted_iota(jnp.int32, (chunk, cols), 1)

    def wide(x):
        return jnp.concatenate([x] * (cols // 128), axis=1) if cols > 128 else x

    def softmax(at):
        target_at = wide(column[at, :])
        score = [scores[g, at, :] * inv_scale for g in range(parts)]
        top = score[0]
        for g in range(1, parts):
            top = jnp.maximum(top, score[g])
        top = jnp.max(top, axis=1, keepdims=True)
        expo = [jnp.exp(s - top) for s in score]
        total = expo[0]
        for g in range(1, parts):
            total = total + expo[g]
        total = jnp.sum(total, axis=1, keepdims=True)
        scale = 1.0 / total
        target = jnp.zeros((chunk, cols), jnp.float32)
        for g in range(parts):
            onehot = lane + g * cols == target_at
            target = target + jnp.where(onehot, score[g], 0.0)
            dz[g, at, :] = (expo[g] * scale - jnp.where(onehot, 1.0, 0.0)).astype(dz.dtype)
        target = jnp.sum(target, axis=1, keepdims=True)
        loss_acc[...] += (top + jnp.log(total)) - target + jnp.zeros_like(loss_acc)

    def encode(way, g, c, value):
        here = pl.ds(pl.multiple_of(c * chunk, chunk), chunk)
        gain = wide(CODE_MAX / bound_out[way, g, 0:1, :])
        code = (value * gain + ROUND) - ROUND
        outgo[way, g, here, :] = code.astype(jnp.int32).astype(outgo.dtype)

    def decode(way, g, c):
        here = pl.ds(pl.multiple_of(c * chunk, chunk), chunk)
        if not coded:
            return partial[way, g, here, :]
        gain = wide(bound_in[way, g, 0:1, :] * (1.0 / CODE_MAX))
        return partial[way, g, here, :].astype(jnp.int32).astype(jnp.float32) * gain

    def new_block(way, g, pos):
        these = pl.ds(rows_of(way, 0), half)
        block = lax.dot_general(
            emb[these, :], tiles[g], (((1,), (1,)), ((), ())), preferred_element_type=jnp.float32
        )
        scores[g, these, :] = block
        if not coded:
            return
        biggest = jnp.max(jnp.max(jnp.abs(block), axis=0, keepdims=True), axis=1, keepdims=True)
        biggest = jnp.broadcast_to(biggest, (8, 128))

        @pl.when(pos == 0)
        def _():
            bound_out[way, g] = jnp.maximum(biggest, 1e-20)

        @pl.when(pos > 0)
        def _():
            bound_copy(way, g).wait_recv()
            bound_out[way, g] = bound_in[way, g] + biggest

        @pl.when(pos < last)
        def _():
            bound_copy(way, g).start()
            bound_top[...] = jnp.maximum(bound_top[...], bound_out[way, g])

    dz_start = (parts - 1) * chunks + LAG * last
    tail_start = ratio * dz_chunks
    ret_start = dz_start + tail_start + DZ_LAG * last
    steps = ret_start + (parts - 1) * dz_chunks + 1

    def send_pieces(q):
        out = lax.dot_general(
            dz[q], emb[...], (((0,), (0,)), ((), ())), preferred_element_type=jnp.float32
        ).astype(piece.dtype)
        for j in range(list_len):
            piece[j] = out[j * piece_rows : (j + 1) * piece_rows, :]
        for k in range(1, groups):
            to = lax.rem(me + k, groups)
            for t in range(CAP):
                ret[q, to * CAP + t] = piece[back[to * CAP + t]]
            ret_copy(q, k).start()
        for t in range(CAP):
            ret[q, me * CAP + t] = piece[back[me * CAP + t]]
        own_ret(q).start()

    def step(i, carry):
        for g in range(parts):

            @pl.when(i == 2 * g * chunks)
            def _():
                tiles_in(g)

        way = lax.rem(i, 2)
        s = i // 2
        q_step = s - ret_start

        @pl.when((way == 0) & (q_step >= 0) & (lax.rem(q_step, dz_chunks) == 0))
        def _():
            send_pieces(q_step // dz_chunks)

        pos = jnp.where(way == 0, z, last - z)
        turn = s - LAG * pos

        @pl.when((turn >= 0) & (turn < parts * chunks))
        def _():
            g = turn // chunks
            c = lax.rem(turn, chunks)

            @pl.when(c == 0)
            def _():
                new_block(way, g, pos)

            at = pl.ds(rows_of(way, c * chunk), chunk)

            @pl.when(pos == 0)
            def _():
                if coded:
                    encode(way, g, c, scores[g, at, :])
                part_copy(way, g, c, True).start()

            @pl.when((pos > 0) & (pos < last))
            def _():
                part_copy(way, g, c, False).wait_recv()
                value = decode(way, g, c) + scores[g, at, :]
                if coded:
                    encode(way, g, c, value)
                else:
                    partial[way, g, pl.ds(pl.multiple_of(c * chunk, chunk), chunk), :] = value
                part_copy(way, g, c, False).start()

            @pl.when(pos == last)
            def _():
                part_copy(way, g, c, False).wait_recv()
                scores[g, at, :] += decode(way, g, c)

            @pl.when((pos == last) & (g == parts - 1))
            def _():
                softmax(at)

        d = s - dz_start - DZ_LAG * (last - pos)
        u = jnp.where(d < tail_start, d // ratio, d - tail_start + dz_chunks)
        now = (d >= 0) & (u < parts * dz_chunks)
        now = now & ((d >= tail_start) | (lax.rem(d + ratio, ratio) == ratio - 1))

        @pl.when(now & (pos < last))
        def _():
            dz_copy(way, u).wait_recv()

        @pl.when(now & (pos > 0))
        def _():
            dz_copy(way, u).start()

        return carry

    lax.fori_loop(0, 2 * steps, step, 0)

    mine = jnp.broadcast_to(jnp.sum(loss_acc[...], axis=0, keepdims=True), (8, 128))
    too_big = jnp.where(bound_top[...] * inv_scale > 48.0, 1.0, 0.0)
    loss_mine[...] = jnp.where(lax.broadcasted_iota(jnp.int32, (8, 128), 0) < 4, mine, too_big)

    def lp_copy(k):
        return pltpu.make_async_remote_copy(
            src_ref=loss_mine,
            dst_ref=loss_plane.at[me],
            send_sem=lp_send.at[k],
            recv_sem=lp_recv.at[k],
            device_id={"proto": lax.rem(me + k, groups)},
            device_id_type=MESH,
        )

    for k in range(1, groups):
        lp_copy(k).start()

    block = 256

    def grad_block(i, carry):
        at = pl.ds(pl.multiple_of(i * block, block), block)
        total = jnp.dot(dz[0, at, :], tiles[0], preferred_element_type=jnp.float32)
        for g in range(1, parts):
            total = total + jnp.dot(dz[g, at, :], tiles[g], preferred_element_type=jnp.float32)
        grad[at, :] = total.astype(grad.dtype)
        return carry

    lax.fori_loop(0, rows // block, grad_block, 0)
    save_grad = pltpu.make_async_copy(grad, grad_hbm, grad_sem)
    save_grad.start()

    loss_plane[me] = loss_mine[...]
    for k in range(1, groups):
        lp_copy(k).wait()
    plane = loss_plane[0]
    for k in range(1, groups):
        plane = plane + loss_plane[k]
    loss_sum[...] = plane

    def lz_copy(k):
        return pltpu.make_async_remote_copy(
            src_ref=loss_sum,
            dst_ref=loss_z.at[z],
            send_sem=lz_send.at[k],
            recv_sem=lz_recv.at[k],
            device_id={"dp": lax.rem(z + k, dp_count)},
            device_id_type=MESH,
        )

    for k in range(1, dp_count):
        lz_copy(k).start()
    loss_z[z] = plane
    for k in range(1, dp_count):
        lz_copy(k).wait()
    whole = loss_z[0]
    for k in range(1, dp_count):
        whole = whole + loss_z[k]
    loss_out[...] = whole * (1.0 / (rows * groups))

    def drain_parts(i, carry):
        way = lax.rem(i, 2)
        turn = i // 2

        @pl.when(jnp.where(way == 0, z, last - z) < last)
        def _():
            part_copy(way, turn // chunks, lax.rem(turn, chunks), False).wait_send()

        return carry

    lax.fori_loop(0, 2 * parts * chunks, drain_parts, 0)

    def drain_dz(i, carry):
        way = lax.rem(i, 2)

        @pl.when(jnp.where(way == 0, z, last - z) > 0)
        def _():
            dz_copy(way, i // 2).wait_send()

        return carry

    lax.fori_loop(0, 2 * parts * dz_chunks, drain_dz, 0)
    if coded:

        def drain_bounds(i, carry):
            way = lax.rem(i, 2)

            @pl.when(jnp.where(way == 0, z, last - z) < last)
            def _():
                bound_copy(way, i // 2).wait_send()

            return carry

        lax.fori_loop(0, 2 * parts, drain_bounds, 0)
    save_grad.wait()

    def drain_ret(q, carry):
        own_ret(q).wait()
        for k in range(1, groups):
            ret_copy(q, k).wait()
        return carry

    lax.fori_loop(0, parts, drain_ret, 0)


def run_main(coded, lists, labels, embeddings, table):
    block_rows, width = embeddings.shape
    list_len = lists.shape[1]
    tiles_here = table.shape[0] // TILE
    groups = lax.axis_size("proto")
    dp_count = lax.axis_size("dp")
    slots = groups * CAP
    cols = list_len * TILE // PARTS
    piece_rows = TILE // PARTS
    half = block_rows // 2
    chunks = half // CHUNK[coded]
    dz_chunks = half // DZ_CHUNK
    bf16, f32, i32 = jnp.bfloat16, jnp.float32, jnp.int32
    dma = pltpu.SemaphoreType.DMA
    vmem = pl.BlockSpec(memory_space=pltpu.VMEM)
    smem = pl.BlockSpec(memory_space=pltpu.SMEM)
    hbm = pl.BlockSpec(memory_space=pltpu.HBM)
    wire = (2, PARTS, half, cols)
    small = (2, PARTS, 8, 128)
    return pl.pallas_call(
        functools.partial(main_kernel, coded, groups, dp_count, tiles_here),
        out_shape=(
            jax.ShapeDtypeStruct((block_rows, width), bf16),
            jax.ShapeDtypeStruct((slots, TILE, width), bf16),
            jax.ShapeDtypeStruct((8, 128), f32),
        ),
        in_specs=[smem, vmem, hbm, hbm],
        out_specs=(hbm, hbm, vmem),
        scratch_shapes=[
            pltpu.VMEM((tiles_here, TILE, width), bf16),
            pltpu.VMEM((block_rows, width), bf16),
            pltpu.VMEM((PARTS, slots, piece_rows, width), bf16),
            pltpu.VMEM((PARTS, cols, width), bf16),
            pltpu.VMEM((PARTS, block_rows, cols), f32),
            pltpu.VMEM(wire, jnp.int16 if coded else f32),
            pltpu.VMEM(wire if coded else (2, PARTS, 16, cols), jnp.int16),
            pltpu.VMEM(small, f32),
            pltpu.VMEM(small, f32),
            pltpu.VMEM((8, 128), f32),
            pltpu.VMEM((block_rows, 128), i32),
            pltpu.VMEM((PARTS, block_rows, cols), bf16),
            pltpu.VMEM((list_len, piece_rows, width), bf16),
            pltpu.VMEM((PARTS, slots, piece_rows, width), bf16),
            pltpu.VMEM((block_rows, width), bf16),
            pltpu.VMEM((CHUNK[coded], 128), f32),
            pltpu.VMEM((8, 128), f32),
            pltpu.VMEM((groups, 8, 128), f32),
            pltpu.VMEM((8, 128), f32),
            pltpu.VMEM((dp_count, 8, 128), f32),
            pltpu.SMEM((slots,), i32),
            pltpu.SMEM((list_len,), i32),
            pltpu.SMEM((slots,), i32),
            dma,
            dma,
            dma,
            dma((PARTS, groups)),
            dma((PARTS, groups)),
            dma((2, PARTS, chunks)),
            dma((2, PARTS, chunks)),
            dma((2, PARTS)),
            dma((2, PARTS)),
            dma((2, PARTS * dz_chunks)),
            dma((2, PARTS * dz_chunks)),
            dma((PARTS, groups)),
            dma((PARTS, groups)),
            dma((PARTS,)),
            dma((groups,)),
            dma((groups,)),
            dma((dp_count,)),
            dma((dp_count,)),
        ]
        + [pltpu.VMEM((slots, piece_rows, width), bf16)] * PARTS,
        compiler_params=pltpu.CompilerParams(
            collective_id=int(coded), has_side_effects=True, vmem_limit_bytes=VMEM_LIMIT
        ),
    )(lists, labels.reshape(block_rows // 128, 128), embeddings, table.reshape(tiles_here, TILE, width))


def fused_body(embeddings, table, tile_lists, labels):
    tiles_here = table.shape[0] // TILE

    def finish(grad_emb, returned, loss):
        return place_tiles(tile_lists, returned, grad_emb, loss, tiles_here)

    grad_table, grad_emb, loss = finish(*run_main(CODED, tile_lists, labels, embeddings, table))
    return (loss.reshape(()), grad_emb, grad_table.reshape(table.shape))


def any_body(embeddings, table, tile_lists, labels):
    block_rows, width = embeddings.shape
    cols = tile_lists.shape[1] * TILE
    need = block_rows * cols * (4 + 4 + 2 + 2) + 2 * table.shape[0] * width * 2
    if need + 8 * 2**20 <= VMEM_LIMIT and block_rows % 1024 == 0:
        return fused_body(embeddings, table, tile_lists, labels)
    return body(embeddings, table, tile_lists, labels)


def solution(mesh):
    placed = (P("proto", "dp"), P("proto", "dp"), P(), P("proto"))
    return jax.shard_map(
        any_body,
        mesh=mesh,
        in_specs=placed,
        out_specs=(P(), P("proto", "dp"), P("proto", "dp")),
        check_vma=False,
    )
```

```python
import functools
import math

import jax
import jax.numpy as jnp
from jax import lax
from jax.experimental import pallas as pl
from jax.experimental.pallas import tpu as pltpu
from jax.sharding import PartitionSpec as P

D = 2560
TILE = 128
CAP = 2
PARTS = 4
CHUNK = {False: 64, True: 128}
DZ_CHUNK = 128
LAG = 4
DZ_LAG = 4
CODE_MAX = 32766.0
GUARD = 1
BOUND = 48.0
SOFT = 32
ROUND = 12582912.0
VMEM_LIMIT = 56 * 2**20
MESH = pl.DeviceIdType.MESH


def slot_plan(ids, tiles_here):
    owners = ids // tiles_here
    local = ids % tiles_here
    count = ids.shape[-1]
    before = jnp.arange(count)[:, None] > jnp.arange(count)[None, :]
    earlier = (owners[..., :, None] == owners[..., None, :]) & before
    rank = jnp.sum(earlier.astype(jnp.int32), axis=-1)
    return (owners, local, rank)


def softmax_terms(scores, ids, lab, list_len):
    hit = (ids[None, :] == (lab // TILE)[:, None]).astype(jnp.int32)
    column = (
        jnp.sum(hit * (jnp.arange(list_len, dtype=jnp.int32) * TILE)[None, :], axis=1) + lab % TILE
    )
    onehot = (jnp.arange(list_len * TILE, dtype=jnp.int32)[None, :] == column[:, None]).astype(
        jnp.float32
    )
    top = jnp.max(scores, axis=1, keepdims=True)
    expo = jnp.exp(scores - top)
    total = jnp.sum(expo, axis=1, keepdims=True)
    lse = top[:, 0] + jnp.log(total[:, 0])
    target = jnp.sum(scores * onehot, axis=1)
    dz_rows = (expo / total - onehot).astype(jnp.bfloat16)
    return (jnp.sum(lse - target), dz_rows)


def body(embeddings, table, tile_lists, labels):
    block_rows, width = embeddings.shape
    list_len = tile_lists.shape[1]
    tiles_here = table.shape[0] // TILE
    groups = lax.axis_size("proto")
    dp_count = lax.axis_size("dp")
    rows_dev = block_rows // dp_count
    total_rows = block_rows * groups
    me = lax.axis_index("proto")
    part = lax.axis_index("dp")
    inv_scale = 1.0 / math.sqrt(D)
    owners, local, rank = slot_plan(tile_lists, tiles_here)
    match = (owners == me)[:, :, None] & (
        rank[:, :, None] == jnp.arange(CAP, dtype=jnp.int32)[None, None, :]
    )
    select = jnp.sum(match.astype(jnp.int32) * local[:, :, None], axis=1)
    shaped_table = table.reshape(tiles_here, TILE, width)
    outgoing = pack_tiles(shaped_table, select.reshape(-1)).reshape(groups, CAP, TILE, width)
    incoming = lax.all_to_all(outgoing, "proto", split_axis=0, concat_axis=0, tiled=True)
    my_ids = lax.dynamic_index_in_dim(tile_lists, me, 0, keepdims=False)
    my_owner = lax.dynamic_index_in_dim(owners, me, 0, keepdims=False)
    my_rank = lax.dynamic_index_in_dim(rank, me, 0, keepdims=False)
    flat_slot = my_owner * CAP + my_rank
    tiles = pack_tiles(incoming.reshape(groups * CAP, TILE, width), flat_slot).reshape(
        list_len * TILE, width
    )
    scores = (
        lax.psum_scatter(
            lax.dot_general(
                embeddings, tiles, (((1,), (1,)), ((), ())), preferred_element_type=jnp.float32
            ),
            "dp",
            scatter_dimension=0,
            tiled=True,
        )
        * inv_scale
    )
    my_labels = lax.dynamic_slice_in_dim(labels, part * rows_dev, rows_dev, 0)
    loss_part, dz_rows = softmax_terms(scores, my_ids, my_labels, list_len)
    dz_block = lax.all_gather(dz_rows, "dp", axis=0, tiled=True)
    loss = lax.psum(loss_part, ("dp", "proto")) / total_rows
    grad_emb = jnp.dot(dz_block, tiles, preferred_element_type=jnp.float32).astype(jnp.bfloat16)
    piece = lax.dot_general(
        dz_block, embeddings, (((0,), (0,)), ((), ())), preferred_element_type=jnp.float32
    ).astype(jnp.bfloat16)
    returning = (
        jnp.zeros((groups * CAP, TILE, width), jnp.bfloat16)
        .at[flat_slot]
        .set(piece.reshape(list_len, TILE, width))
    )
    returned = lax.all_to_all(
        returning.reshape(groups, CAP, TILE, width),
        "proto",
        split_axis=0,
        concat_axis=0,
        tiled=True,
    )
    accum = (
        jnp.zeros((tiles_here, TILE, width), jnp.float32)
        .at[select.reshape(-1)]
        .add(returned.reshape(groups * CAP, TILE, width))
    )
    grad_table = accum.reshape(tiles_here * TILE, width).astype(jnp.bfloat16)
    return (loss, grad_emb, grad_table)


def pack_kernel(pick_ref, table_ref, out_ref, sems):
    count = out_ref.shape[0]

    def copy(slot):
        return pltpu.make_async_copy(
            table_ref.at[pick_ref[slot]], out_ref.at[slot], sems.at[slot]
        )

    for slot in range(count):
        copy(slot).start()
    for slot in range(count):
        copy(slot).wait()


def pack_tiles(shaped_table, pick):
    count = pick.shape[0]
    _, tile, width = shaped_table.shape
    return pl.pallas_call(
        pack_kernel,
        out_shape=jax.ShapeDtypeStruct((count, tile, width), shaped_table.dtype),
        grid_spec=pltpu.PrefetchScalarGridSpec(
            num_scalar_prefetch=1,
            grid=(1,),
            in_specs=[pl.BlockSpec(memory_space=pl.ANY)],
            out_specs=pl.BlockSpec(memory_space=pltpu.VMEM),
            scratch_shapes=[pltpu.SemaphoreType.DMA((count,))],
        ),
        compiler_params=pltpu.CompilerParams(vmem_limit_bytes=32 * 2**20),
    )(pick, shaped_table)


def place_kernel(plan, returned, emb_in, loss_in, table_out, emb_out, loss_out, got, emb, zero, sums, in_sem, emb_sem, out_sem):
    tiles_here = table_out.shape[0]
    count = returned.shape[0]
    load = pltpu.make_async_copy(returned, got, in_sem)
    load.start()
    load_emb = pltpu.make_async_copy(emb_in, emb, emb_sem)
    load_emb.start()
    zero[...] = jnp.zeros_like(zero)

    def from_zero(t):
        return pltpu.make_async_copy(zero, table_out.at[t], out_sem.at[t])

    def from_slot(t):
        return pltpu.make_async_copy(got.at[plan[1, t]], table_out.at[t], out_sem.at[t])

    for t in range(tiles_here):

        @pl.when(plan[0, t] == 0)
        def _():
            from_zero(t).start()

    load_emb.wait()
    save_emb = pltpu.make_async_copy(emb, emb_out, emb_sem)
    save_emb.start()
    load.wait()
    for t in range(tiles_here):

        @pl.when(plan[0, t] == 1)
        def _():
            from_slot(t).start()

    def many(t, carry):
        @pl.when(plan[0, t] == 2)
        def _():
            sums[...] = got[plan[1, t]].astype(jnp.float32) + got[plan[2, t]].astype(jnp.float32)

        @pl.when(plan[0, t] > 2)
        def _():
            sums[...] = jnp.zeros_like(sums)

            def add(slot, carry):
                @pl.when(plan[3, slot] == t)
                def _():
                    sums[...] += got[slot].astype(jnp.float32)

                return carry

            lax.fori_loop(0, count, add, 0)

        @pl.when(plan[0, t] > 1)
        def _():
            got[plan[1, t]] = sums[...].astype(got.dtype)
            from_slot(t).start()

        return carry

    lax.fori_loop(0, tiles_here, many, 0)
    loss_out[0, 0] = jnp.max(loss_in[0:1, :])
    for t in range(tiles_here):
        from_zero(t).wait()
    save_emb.wait()


def place_tiles(plan, returned, grad_emb, loss, tiles_here):
    count, tile, width = returned.shape
    smem = pl.BlockSpec(memory_space=pltpu.SMEM)
    vmem = pl.BlockSpec(memory_space=pltpu.VMEM)
    hbm = pl.BlockSpec(memory_space=pltpu.HBM)
    dma = pltpu.SemaphoreType.DMA
    return pl.pallas_call(
        place_kernel,
        out_shape=(
            jax.ShapeDtypeStruct((tiles_here, tile, width), returned.dtype),
            jax.ShapeDtypeStruct(grad_emb.shape, grad_emb.dtype),
            jax.ShapeDtypeStruct((1, 1), jnp.float32),
        ),
        in_specs=[smem, hbm, hbm, vmem],
        out_specs=(hbm, hbm, smem),
        scratch_shapes=[
            pltpu.VMEM(returned.shape, returned.dtype),
            pltpu.VMEM(grad_emb.shape, grad_emb.dtype),
            pltpu.VMEM((tile, width), returned.dtype),
            pltpu.VMEM((tile, width), jnp.float32),
            dma,
            dma,
            dma((tiles_here,)),
        ],
        compiler_params=pltpu.CompilerParams(vmem_limit_bytes=VMEM_LIMIT),
    )(plan, returned, grad_emb, loss)


def main_kernel(
    coded,
    groups,
    dp_count,
    tiles_here,
    lists,
    labels,
    emb_hbm,
    table_hbm,
    grad_hbm,
    returned,
    loss_out,
    plan_out,
    table,
    emb,
    out_tiles,
    tiles,
    scores,
    partial,
    outgo,
    bound_in,
    bound_out,
    bound_own,
    bound_top,
    column,
    dz,
    piece,
    ret,
    grad,
    loss_acc,
    loss_mine,
    loss_plane,
    loss_sum,
    loss_z,
    select,
    my_slot,
    back,
    table_sem,
    emb_sem,
    grad_sem,
    tile_send,
    tile_recv,
    part_send,
    part_recv,
    bound_send,
    bound_recv,
    dz_send,
    dz_recv,
    ret_send,
    ret_recv,
    own_ret_sem,
    lp_send,
    lp_recv,
    lz_send,
    lz_recv,
    *incoming,
):
    me = lax.axis_index("proto")
    z = lax.axis_index("dp")
    rows, width = emb.shape
    list_len = lists.shape[1]
    parts, cols, _ = tiles.shape
    piece_rows = TILE // parts
    chunk = CHUNK[coded]
    half = rows // 2
    chunks = half // chunk
    dz_chunks = half // DZ_CHUNK
    ratio = DZ_CHUNK // chunk
    last = dp_count - 1
    block = 256
    inv_scale = 1.0 / math.sqrt(D)

    barrier = pltpu.get_barrier_semaphore()
    for k in range(1, groups):
        pl.semaphore_signal(
            barrier, inc=1, device_id={"proto": lax.rem(me + k, groups)}, device_id_type=MESH
        )
    for k in range(1, dp_count):
        pl.semaphore_signal(
            barrier, inc=1, device_id={"dp": lax.rem(z + k, dp_count)}, device_id_type=MESH
        )
    load_table = pltpu.make_async_copy(table_hbm, table, table_sem)
    load_table.start()
    load_emb = pltpu.make_async_copy(emb_hbm, emb, emb_sem)
    load_emb.start()

    base = me * tiles_here
    lane_one = lax.broadcasted_iota(jnp.int32, (1, 128), 1)
    count = jnp.zeros((1, 128), jnp.int32)
    first, second, held = count, count, count
    for b in range(groups):
        local = [lists[b, j] - base for j in range(list_len)]
        mine = [(t >= 0) & (t < tiles_here) for t in local]
        low, high = jnp.int32(0), jnp.int32(0)
        for j in range(list_len):
            high = jnp.where(mine[j], local[j], high)
            back_j = list_len - 1 - j
            low = jnp.where(mine[back_j], local[back_j], low)
        select[b * CAP] = low
        select[b * CAP + 1] = high
        listed = mine[0]
        for j in range(1, list_len):
            listed = listed | mine[j]
        for t, tile in enumerate((low, high)):
            slot = b * CAP + t
            tile = jnp.where(listed, tile, -1)
            hit = lane_one == tile
            count = count + jnp.where(hit, 1, 0)
            second = jnp.where(hit, first, second)
            first = jnp.where(hit, slot, first)
            held = jnp.where(lane_one == slot, tile, held)
    plan_out[0:1, :] = count
    plan_out[1:2, :] = first
    plan_out[2:3, :] = second
    plan_out[3:4, :] = held
    plan_out[4:8, :] = jnp.zeros((4, 128), jnp.int32)

    load_table.wait()
    for k in range(groups):
        to = lax.rem(me + k, groups)
        for t in range(CAP):
            slot = to * CAP + t
            for g in range(parts):
                tile = table[select[slot], g * piece_rows : (g + 1) * piece_rows, :]
                if k == 0:
                    incoming[g][slot] = tile
                else:
                    out_tiles[g, slot] = tile
    pl.semaphore_wait(barrier, groups + dp_count - 2)

    def tile_copy(g, k):
        to = lax.rem(me + k, groups)
        return pltpu.make_async_remote_copy(
            src_ref=out_tiles.at[g, pl.ds(to * CAP, CAP)],
            dst_ref=incoming[g].at[pl.ds(me * CAP, CAP)],
            send_sem=tile_send.at[g, k],
            recv_sem=tile_recv.at[g, k],
            device_id={"proto": to},
            device_id_type=MESH,
        )

    core = lax.rem(me, 2)
    for first in range(2):
        for g in range(parts):
            for a in range(groups // 2):
                k = lax.rem(2 * a + first - core + groups, groups)
                if a > 0:
                    tile_copy(g, k).start()
                else:

                    @pl.when(core != first)
                    def _():
                        tile_copy(g, k).start()

    ids = [lists[me, j] for j in range(list_len)]
    owner = [lax.div(t, jnp.int32(tiles_here)) for t in ids]
    flat = []
    for j in range(list_len):
        rank = jnp.int32(0)
        for i in range(j):
            rank = rank + jnp.where(owner[i] == owner[j], 1, 0)
        flat.append(owner[j] * CAP + rank)
        my_slot[j] = flat[j]
    for s in range(groups * CAP):
        at = jnp.int32(0)
        for j in range(1, list_len):
            at = jnp.where(flat[j] == s, j, at)
        back[s] = at
    lab = labels[...]
    lab_tile = lax.shift_right_logical(lab, 7)
    within = lax.bitwise_and(lab, TILE - 1)
    part_of = lax.shift_right_logical(within, int(math.log2(piece_rows)))
    where_to = part_of * cols + lax.bitwise_and(within, piece_rows - 1)
    for j in range(list_len):
        where_to = where_to + jnp.where(lab_tile == ids[j], j * piece_rows, 0)
    for i in range(rows // 128):
        column[i * 128 : (i + 1) * 128, :] = jnp.broadcast_to(where_to[i : i + 1, :], (128, 128)).T

    loss_acc[...] = jnp.zeros_like(loss_acc)
    bound_top[...] = jnp.zeros_like(bound_top)
    load_emb.wait()

    def tiles_in(g):
        for k in range(1, groups):
            tile_copy(g, k).wait_recv()
        for j in range(list_len):
            tiles[g, j * piece_rows : (j + 1) * piece_rows, :] = incoming[g][my_slot[j]]

    def rows_of(way, at):
        return pl.multiple_of((1 - way) * half + at, 32)

    def part_copy(way, g, c, first):
        here = pl.ds(pl.multiple_of(c * chunk, chunk), chunk)
        dst = partial.at[way, g, here]
        if coded:
            src = outgo.at[way, g, here]
        elif first:
            src = scores.at[g, pl.ds(rows_of(way, c * chunk), chunk)]
        else:
            src = dst
        return pltpu.make_async_remote_copy(
            src_ref=src,
            dst_ref=dst,
            send_sem=part_send.at[way, g, c],
            recv_sem=part_recv.at[way, g, c],
            device_id={"dp": jnp.clip(z + 1 - 2 * way, 0, last)},
            device_id_type=MESH,
        )

    def bound_copy(way, g):
        return pltpu.make_async_remote_copy(
            src_ref=bound_out.at[way, g],
            dst_ref=bound_in.at[way, g],
            send_sem=bound_send.at[way, g],
            recv_sem=bound_recv.at[way, g],
            device_id={"dp": jnp.clip(z + 1 - 2 * way, 0, last)},
            device_id_type=MESH,
        )

    def dz_copy(way, u):
        at = dz.at[u // dz_chunks, pl.ds(rows_of(way, lax.rem(u, dz_chunks) * DZ_CHUNK), DZ_CHUNK)]
        return pltpu.make_async_remote_copy(
            src_ref=at,
            dst_ref=at,
            send_sem=dz_send.at[way, u],
            recv_sem=dz_recv.at[way, u],
            device_id={"dp": jnp.clip(z - 1 + 2 * way, 0, last)},
            device_id_type=MESH,
        )

    def ret_copy(q, k):
        to = lax.rem(me + k, groups)
        return pltpu.make_async_remote_copy(
            src_ref=ret.at[q, pl.ds(to * CAP, CAP)],
            dst_ref=returned.at[pl.ds(me * CAP, CAP), pl.ds(pl.multiple_of(q * piece_rows, 16), piece_rows)],
            send_sem=ret_send.at[q, k],
            recv_sem=ret_recv.at[q, k],
            device_id={"proto": to},
            device_id_type=MESH,
        )

    def own_ret(q):
        return pltpu.make_async_copy(
            ret.at[q, pl.ds(me * CAP, CAP)],
            returned.at[pl.ds(me * CAP, CAP), pl.ds(pl.multiple_of(q * piece_rows, 16), piece_rows)],
            own_ret_sem.at[q],
        )

    lane = lax.broadcasted_iota(jnp.int32, (SOFT, cols), 1)

    def wide(x):
        return jnp.concatenate([x] * (cols // 128), axis=1) if cols > 128 else x

    def softmax_rows(i, start):
        at = pl.ds(pl.multiple_of(start + i * SOFT, SOFT), SOFT)
        target_at = wide(column[at, :])
        score = [scores[g, at, :] * inv_scale for g in range(parts)]
        top = score[0]
        for g in range(1, parts):
            top = jnp.maximum(top, score[g])
        top = jnp.max(top, axis=1, keepdims=True)
        expo = [jnp.exp(s - top) for s in score]
        total = expo[0]
        for g in range(1, parts):
            total = total + expo[g]
        total = jnp.sum(total, axis=1, keepdims=True)
        scale = 1.0 / total
        target = jnp.zeros((SOFT, cols), jnp.float32)
        for g in range(parts):
            onehot = lane + g * cols == target_at
            target = target + jnp.where(onehot, score[g], 0.0)
            dz[g, at, :] = (expo[g] * scale - jnp.where(onehot, 1.0, 0.0)).astype(dz.dtype)
        target = jnp.sum(target, axis=1, keepdims=True)
        loss_acc[...] += (top + jnp.log(total)) - target + jnp.zeros_like(loss_acc)
        return start

    def encode(way, g, c, value):
        here = pl.ds(pl.multiple_of(c * chunk, chunk), chunk)
        gain = wide(CODE_MAX / bound_out[way, g, 0:1, :])
        code = (value * gain + ROUND) - ROUND
        outgo[way, g, here, :] = code.astype(jnp.int32).astype(outgo.dtype)

    def decode(way, g, c):
        here = pl.ds(pl.multiple_of(c * chunk, chunk), chunk)
        if not coded:
            return partial[way, g, here, :]
        gain = wide(bound_in[way, g, 0:1, :] * (1.0 / CODE_MAX))
        return partial[way, g, here, :].astype(jnp.int32).astype(jnp.float32) * gain

    def new_block(g):
        biggest = []
        for r in range(rows // block):
            these = slice(r * block, (r + 1) * block)
            value = lax.dot_general(
                emb[these, :], tiles[g], (((1,), (1,)), ((), ())), preferred_element_type=jnp.float32
            )
            scores[g, these, :] = value
            if coded:
                biggest.append(jnp.max(jnp.abs(value), axis=0, keepdims=True))
        if coded:
            per_way = len(biggest) // 2
            for way in range(2):
                some = biggest[(1 - way) * per_way : (2 - way) * per_way]
                top = some[0]
                for x in some[1:]:
                    top = jnp.maximum(top, x)
                top = jnp.max(top, axis=1, keepdims=True)
                bound_own[way, g] = jnp.broadcast_to(jnp.maximum(top, 1e-20), (8, 128))

    def new_bound(way, g, pos):
        @pl.when(pos == 0)
        def _():
            bound_out[way, g] = bound_own[way, g]

        @pl.when(pos > 0)
        def _():
            bound_copy(way, g).wait_recv()
            bound_out[way, g] = bound_in[way, g] + bound_own[way, g]

        @pl.when(pos < last)
        def _():
            bound_copy(way, g).start()
            bound_top[...] = jnp.maximum(bound_top[...], bound_out[way, g])

    dz_start = (parts - 1) * chunks + LAG * last
    tail_start = ratio * dz_chunks
    ret_start = dz_start + tail_start + DZ_LAG * last
    steps = ret_start + (parts - 1) * dz_chunks + 1

    def send_pieces(q):
        out = lax.dot_general(
            dz[q], emb[...], (((0,), (0,)), ((), ())), preferred_element_type=jnp.float32
        ).astype(piece.dtype)
        for j in range(list_len):
            piece[j] = out[j * piece_rows : (j + 1) * piece_rows, :]
        for k in range(1, groups):
            to = lax.rem(me + k, groups)
            for t in range(CAP):
                ret[q, to * CAP + t] = piece[back[to * CAP + t]]
            ret_copy(q, k).start()
        for t in range(CAP):
            ret[q, me * CAP + t] = piece[back[me * CAP + t]]
        own_ret(q).start()

    def lp_copy(k):
        return pltpu.make_async_remote_copy(
            src_ref=loss_mine,
            dst_ref=loss_plane.at[me],
            send_sem=lp_send.at[k],
            recv_sem=lp_recv.at[k],
            device_id={"proto": lax.rem(me + k, groups)},
            device_id_type=MESH,
        )

    def lz_copy(k):
        return pltpu.make_async_remote_copy(
            src_ref=loss_sum,
            dst_ref=loss_z.at[z],
            send_sem=lz_send.at[k],
            recv_sem=lz_recv.at[k],
            device_id={"dp": lax.rem(z + k, dp_count)},
            device_id_type=MESH,
        )

    def loss_begin():
        mine = jnp.broadcast_to(jnp.sum(loss_acc[...], axis=0, keepdims=True), (8, 128))
        too_big = jnp.where(bound_top[...] * inv_scale > BOUND, 1.0, 0.0)
        loss_mine[...] = jnp.where(lax.broadcasted_iota(jnp.int32, (8, 128), 0) < 4, mine, too_big)
        loss_plane[me] = loss_mine[...]
        for k in range(1, groups):
            lp_copy(k).start()

    def loss_middle():
        for k in range(1, groups):
            lp_copy(k).wait()
        plane = loss_plane[0]
        for k in range(1, groups):
            plane = plane + loss_plane[k]
        loss_sum[...] = plane
        loss_z[z] = plane
        for k in range(1, dp_count):
            lz_copy(k).start()

    def loss_end():
        for k in range(1, dp_count):
            lz_copy(k).wait()
        whole = loss_z[0]
        for k in range(1, dp_count):
            whole = whole + loss_z[k]
        loss_out[...] = whole * (1.0 / (rows * groups))

    def step(i, carry):
        for g in range(parts):

            @pl.when(i == 2 * g * chunks)
            def _():
                tiles_in(g)

        way = lax.rem(i, 2)
        s = i // 2

        @pl.when((way == 0) & (s < parts * chunks) & (lax.rem(s, chunks) == 0))
        def _():
            new_block(s // chunks)

        q_step = s - ret_start

        @pl.when((way == 0) & (q_step >= 0) & (lax.rem(q_step, dz_chunks) == 0))
        def _():
            send_pieces(q_step // dz_chunks)

        for at, part in enumerate((loss_begin, loss_middle, loss_end)):

            @pl.when((way == 0) & (q_step == at * dz_chunks))
            def _():
                part()

        pos = jnp.where(way == 0, z, last - z)
        turn = s - LAG * pos

        @pl.when((turn >= 0) & (turn < parts * chunks))
        def _():
            g = turn // chunks
            c = lax.rem(turn, chunks)

            if coded:

                @pl.when(c == 0)
                def _():
                    new_bound(way, g, pos)

            at = pl.ds(rows_of(way, c * chunk), chunk)

            @pl.when(pos == 0)
            def _():
                if coded:
                    encode(way, g, c, scores[g, at, :])
                part_copy(way, g, c, True).start()

            @pl.when((pos > 0) & (pos < last))
            def _():
                part_copy(way, g, c, False).wait_recv()
                value = decode(way, g, c) + scores[g, at, :]
                if coded:
                    encode(way, g, c, value)
                else:
                    partial[way, g, pl.ds(pl.multiple_of(c * chunk, chunk), chunk), :] = value
                part_copy(way, g, c, False).start()

            @pl.when(pos == last)
            def _():
                part_copy(way, g, c, False).wait_recv()
                scores[g, at, :] += decode(way, g, c)

            @pl.when((pos == last) & (g == parts - 1))
            def _():
                lax.fori_loop(0, chunk // SOFT, softmax_rows, rows_of(way, c * chunk))

        d = s - dz_start - DZ_LAG * (last - pos)
        u = jnp.where(d < tail_start, d // ratio, d - tail_start + dz_chunks)
        now = (d >= 0) & (u < parts * dz_chunks)
        now = now & ((d >= tail_start) | (lax.rem(d + ratio, ratio) == ratio - 1))

        @pl.when(now & (pos < last))
        def _():
            dz_copy(way, u).wait_recv()

        @pl.when(now & (pos > 0))
        def _():
            dz_copy(way, u).start()

        return carry

    lax.fori_loop(0, 2 * steps, step, 0)

    def save_grad(i):
        at = pl.ds(pl.multiple_of(i * block, block), block)
        return pltpu.make_async_copy(grad.at[at], grad_hbm.at[at], grad_sem.at[i])

    def grad_block(i, carry):
        at = pl.ds(pl.multiple_of(i * block, block), block)
        total = jnp.dot(dz[0, at, :], tiles[0], preferred_element_type=jnp.float32)
        for g in range(1, parts):
            total = total + jnp.dot(dz[g, at, :], tiles[g], preferred_element_type=jnp.float32)
        grad[at, :] = total.astype(grad.dtype)
        save_grad(i).start()
        return carry

    lax.fori_loop(0, rows // block, grad_block, 0)

    def drain_parts(i, carry):
        way = lax.rem(i, 2)
        turn = i // 2

        @pl.when(jnp.where(way == 0, z, last - z) < last)
        def _():
            part_copy(way, turn // chunks, lax.rem(turn, chunks), False).wait_send()

        return carry

    lax.fori_loop(0, 2 * parts * chunks, drain_parts, 0)

    def drain_dz(i, carry):
        way = lax.rem(i, 2)

        @pl.when(jnp.where(way == 0, z, last - z) > 0)
        def _():
            dz_copy(way, i // 2).wait_send()

        return carry

    lax.fori_loop(0, 2 * parts * dz_chunks, drain_dz, 0)
    if coded:

        def drain_bounds(i, carry):
            way = lax.rem(i, 2)

            @pl.when(jnp.where(way == 0, z, last - z) < last)
            def _():
                bound_copy(way, i // 2).wait_send()

            return carry

        lax.fori_loop(0, 2 * parts, drain_bounds, 0)
    for g in range(parts):
        for k in range(1, groups):
            tile_copy(g, k).wait_send()
    for i in range(rows // block):
        save_grad(i).wait()

    def drain_ret(q, carry):
        own_ret(q).wait()
        for k in range(1, groups):
            ret_copy(q, k).wait()
        return carry

    lax.fori_loop(0, parts, drain_ret, 0)


def run_main(coded, lists, labels, embeddings, table):
    block_rows, width = embeddings.shape
    list_len = lists.shape[1]
    tiles_here = table.shape[0] // TILE
    groups = lax.axis_size("proto")
    dp_count = lax.axis_size("dp")
    slots = groups * CAP
    cols = list_len * TILE // PARTS
    piece_rows = TILE // PARTS
    half = block_rows // 2
    chunks = half // CHUNK[coded]
    dz_chunks = half // DZ_CHUNK
    bf16, f32, i32 = jnp.bfloat16, jnp.float32, jnp.int32
    dma = pltpu.SemaphoreType.DMA
    vmem = pl.BlockSpec(memory_space=pltpu.VMEM)
    smem = pl.BlockSpec(memory_space=pltpu.SMEM)
    hbm = pl.BlockSpec(memory_space=pltpu.HBM)
    wire = (2, PARTS, half, cols)
    small = (2, PARTS, 8, 128)
    return pl.pallas_call(
        functools.partial(main_kernel, coded, groups, dp_count, tiles_here),
        out_shape=(
            jax.ShapeDtypeStruct((block_rows, width), bf16),
            jax.ShapeDtypeStruct((slots, TILE, width), bf16),
            jax.ShapeDtypeStruct((8, 128), f32),
            jax.ShapeDtypeStruct((8, 128), i32),
        ),
        in_specs=[smem, vmem, hbm, hbm],
        out_specs=(hbm, hbm, vmem, vmem),
        scratch_shapes=[
            pltpu.VMEM((tiles_here, TILE, width), bf16),
            pltpu.VMEM((block_rows, width), bf16),
            pltpu.VMEM((PARTS, slots, piece_rows, width), bf16),
            pltpu.VMEM((PARTS, cols, width), bf16),
            pltpu.VMEM((PARTS, block_rows, cols), f32),
            pltpu.VMEM(wire, jnp.int16 if coded else f32),
            pltpu.VMEM(wire if coded else (2, PARTS, 16, cols), jnp.int16),
            pltpu.VMEM(small, f32),
            pltpu.VMEM(small, f32),
            pltpu.VMEM(small, f32),
            pltpu.VMEM((8, 128), f32),
            pltpu.VMEM((block_rows, 128), i32),
            pltpu.VMEM((PARTS, block_rows, cols), bf16),
            pltpu.VMEM((list_len, piece_rows, width), bf16),
            pltpu.VMEM((PARTS, slots, piece_rows, width), bf16),
            pltpu.VMEM((block_rows, width), bf16),
            pltpu.VMEM((SOFT, 128), f32),
            pltpu.VMEM((8, 128), f32),
            pltpu.VMEM((groups, 8, 128), f32),
            pltpu.VMEM((8, 128), f32),
            pltpu.VMEM((dp_count, 8, 128), f32),
            pltpu.SMEM((slots,), i32),
            pltpu.SMEM((list_len,), i32),
            pltpu.SMEM((slots,), i32),
            dma,
            dma,
            dma((block_rows // 256,)),
            dma((PARTS, groups)),
            dma((PARTS, groups)),
            dma((2, PARTS, chunks)),
            dma((2, PARTS, chunks)),
            dma((2, PARTS)),
            dma((2, PARTS)),
            dma((2, PARTS * dz_chunks)),
            dma((2, PARTS * dz_chunks)),
            dma((PARTS, groups)),
            dma((PARTS, groups)),
            dma((PARTS,)),
            dma((groups,)),
            dma((groups,)),
            dma((dp_count,)),
            dma((dp_count,)),
        ]
        + [pltpu.VMEM((slots, piece_rows, width), bf16)] * PARTS,
        compiler_params=pltpu.CompilerParams(
            collective_id=int(coded), has_side_effects=True, vmem_limit_bytes=VMEM_LIMIT
        ),
    )(lists, labels.reshape(block_rows // 128, 128), embeddings, table.reshape(tiles_here, TILE, width))


def fused_body(embeddings, table, tile_lists, labels):
    tiles_here = table.shape[0] // TILE
    inputs = (tile_lists, labels, embeddings, table)

    def finish(grad_emb, returned, loss, plan):
        return place_tiles(plan, returned, grad_emb, loss, tiles_here)

    if GUARD == 0:
        grad_table, grad_emb, loss = finish(*run_main(True, *inputs))
    else:
        coded = run_main(True, *inputs)
        grad_table, grad_emb, loss = lax.cond(
            coded[2][7, 0] > 0.0,
            lambda coded, inputs: finish(*run_main(False, *inputs)),
            lambda coded, inputs: finish(*coded),
            coded,
            inputs,
        )
    return (loss.reshape(()), grad_emb, grad_table.reshape(table.shape))


def any_body(embeddings, table, tile_lists, labels):
    block_rows, width = embeddings.shape
    cols = tile_lists.shape[1] * TILE
    need = block_rows * cols * (4 + 4 + 2 + 2) + 2 * table.shape[0] * width * 2
    if need + 8 * 2**20 <= VMEM_LIMIT and block_rows % 1024 == 0:
        return fused_body(embeddings, table, tile_lists, labels)
    return body(embeddings, table, tile_lists, labels)


def solution(mesh):
    placed = (P("proto", "dp"), P("proto", "dp"), P(), P("proto"))
    return jax.shard_map(
        any_body,
        mesh=mesh,
        in_specs=placed,
        out_specs=(P(), P("proto", "dp"), P("proto", "dp")),
        check_vma=False,
    )
```

```python
import functools
import math

import jax
import jax.numpy as jnp
from jax import lax
from jax.experimental import pallas as pl
from jax.experimental.pallas import tpu as pltpu
from jax.sharding import PartitionSpec as P

D = 2560
TILE = 128
CAP = 2
PARTS = 8
CHUNK = {False: 64, True: 256}
DZ_CHUNK = 256
LAG = 4
DZ_LAG = 4
CODE_MAX = 32766.0
GUARD = 1
BOUND = 48.0
SOFT = 32
ROUND = 12582912.0
VMEM_LIMIT = 56 * 2**20
MESH = pl.DeviceIdType.MESH


def slot_plan(ids, tiles_here):
    owners = ids // tiles_here
    local = ids % tiles_here
    count = ids.shape[-1]
    before = jnp.arange(count)[:, None] > jnp.arange(count)[None, :]
    earlier = (owners[..., :, None] == owners[..., None, :]) & before
    rank = jnp.sum(earlier.astype(jnp.int32), axis=-1)
    return (owners, local, rank)


def softmax_terms(scores, ids, lab, list_len):
    hit = (ids[None, :] == (lab // TILE)[:, None]).astype(jnp.int32)
    column = (
        jnp.sum(hit * (jnp.arange(list_len, dtype=jnp.int32) * TILE)[None, :], axis=1) + lab % TILE
    )
    onehot = (jnp.arange(list_len * TILE, dtype=jnp.int32)[None, :] == column[:, None]).astype(
        jnp.float32
    )
    top = jnp.max(scores, axis=1, keepdims=True)
    expo = jnp.exp(scores - top)
    total = jnp.sum(expo, axis=1, keepdims=True)
    lse = top[:, 0] + jnp.log(total[:, 0])
    target = jnp.sum(scores * onehot, axis=1)
    dz_rows = (expo / total - onehot).astype(jnp.bfloat16)
    return (jnp.sum(lse - target), dz_rows)


def body(embeddings, table, tile_lists, labels):
    block_rows, width = embeddings.shape
    list_len = tile_lists.shape[1]
    tiles_here = table.shape[0] // TILE
    groups = lax.axis_size("proto")
    dp_count = lax.axis_size("dp")
    rows_dev = block_rows // dp_count
    total_rows = block_rows * groups
    me = lax.axis_index("proto")
    part = lax.axis_index("dp")
    inv_scale = 1.0 / math.sqrt(D)
    owners, local, rank = slot_plan(tile_lists, tiles_here)
    match = (owners == me)[:, :, None] & (
        rank[:, :, None] == jnp.arange(CAP, dtype=jnp.int32)[None, None, :]
    )
    select = jnp.sum(match.astype(jnp.int32) * local[:, :, None], axis=1)
    shaped_table = table.reshape(tiles_here, TILE, width)
    outgoing = pack_tiles(shaped_table, select.reshape(-1)).reshape(groups, CAP, TILE, width)
    incoming = lax.all_to_all(outgoing, "proto", split_axis=0, concat_axis=0, tiled=True)
    my_ids = lax.dynamic_index_in_dim(tile_lists, me, 0, keepdims=False)
    my_owner = lax.dynamic_index_in_dim(owners, me, 0, keepdims=False)
    my_rank = lax.dynamic_index_in_dim(rank, me, 0, keepdims=False)
    flat_slot = my_owner * CAP + my_rank
    tiles = pack_tiles(incoming.reshape(groups * CAP, TILE, width), flat_slot).reshape(
        list_len * TILE, width
    )
    scores = (
        lax.psum_scatter(
            lax.dot_general(
                embeddings, tiles, (((1,), (1,)), ((), ())), preferred_element_type=jnp.float32
            ),
            "dp",
            scatter_dimension=0,
            tiled=True,
        )
        * inv_scale
    )
    my_labels = lax.dynamic_slice_in_dim(labels, part * rows_dev, rows_dev, 0)
    loss_part, dz_rows = softmax_terms(scores, my_ids, my_labels, list_len)
    dz_block = lax.all_gather(dz_rows, "dp", axis=0, tiled=True)
    loss = lax.psum(loss_part, ("dp", "proto")) / total_rows
    grad_emb = jnp.dot(dz_block, tiles, preferred_element_type=jnp.float32).astype(jnp.bfloat16)
    piece = lax.dot_general(
        dz_block, embeddings, (((0,), (0,)), ((), ())), preferred_element_type=jnp.float32
    ).astype(jnp.bfloat16)
    returning = (
        jnp.zeros((groups * CAP, TILE, width), jnp.bfloat16)
        .at[flat_slot]
        .set(piece.reshape(list_len, TILE, width))
    )
    returned = lax.all_to_all(
        returning.reshape(groups, CAP, TILE, width),
        "proto",
        split_axis=0,
        concat_axis=0,
        tiled=True,
    )
    accum = (
        jnp.zeros((tiles_here, TILE, width), jnp.float32)
        .at[select.reshape(-1)]
        .add(returned.reshape(groups * CAP, TILE, width))
    )
    grad_table = accum.reshape(tiles_here * TILE, width).astype(jnp.bfloat16)
    return (loss, grad_emb, grad_table)


def pack_kernel(pick_ref, table_ref, out_ref, sems):
    count = out_ref.shape[0]

    def copy(slot):
        return pltpu.make_async_copy(
            table_ref.at[pick_ref[slot]], out_ref.at[slot], sems.at[slot]
        )

    for slot in range(count):
        copy(slot).start()
    for slot in range(count):
        copy(slot).wait()


def pack_tiles(shaped_table, pick):
    count = pick.shape[0]
    _, tile, width = shaped_table.shape
    return pl.pallas_call(
        pack_kernel,
        out_shape=jax.ShapeDtypeStruct((count, tile, width), shaped_table.dtype),
        grid_spec=pltpu.PrefetchScalarGridSpec(
            num_scalar_prefetch=1,
            grid=(1,),
            in_specs=[pl.BlockSpec(memory_space=pl.ANY)],
            out_specs=pl.BlockSpec(memory_space=pltpu.VMEM),
            scratch_shapes=[pltpu.SemaphoreType.DMA((count,))],
        ),
        compiler_params=pltpu.CompilerParams(vmem_limit_bytes=32 * 2**20),
    )(pick, shaped_table)


def place_kernel(plan, returned, emb_in, loss_in, table_out, emb_out, loss_out, got, emb, zero, sums, in_sem, emb_sem, out_sem):
    tiles_here = table_out.shape[0]
    count = returned.shape[0]
    load = pltpu.make_async_copy(returned, got, in_sem)
    load.start()
    load_emb = pltpu.make_async_copy(emb_in, emb, emb_sem)
    load_emb.start()
    zero[...] = jnp.zeros_like(zero)

    def from_zero(t):
        return pltpu.make_async_copy(zero, table_out.at[t], out_sem.at[t])

    def from_slot(t):
        return pltpu.make_async_copy(got.at[plan[1, t]], table_out.at[t], out_sem.at[t])

    for t in range(tiles_here):

        @pl.when(plan[0, t] == 0)
        def _():
            from_zero(t).start()

    load_emb.wait()
    save_emb = pltpu.make_async_copy(emb, emb_out, emb_sem)
    save_emb.start()
    load.wait()
    for t in range(tiles_here):

        @pl.when(plan[0, t] == 1)
        def _():
            from_slot(t).start()

    def many(t, carry):
        @pl.when(plan[0, t] == 2)
        def _():
            sums[...] = got[plan[1, t]].astype(jnp.float32) + got[plan[2, t]].astype(jnp.float32)

        @pl.when(plan[0, t] > 2)
        def _():
            sums[...] = jnp.zeros_like(sums)

            def add(slot, carry):
                @pl.when(plan[3, slot] == t)
                def _():
                    sums[...] += got[slot].astype(jnp.float32)

                return carry

            lax.fori_loop(0, count, add, 0)

        @pl.when(plan[0, t] > 1)
        def _():
            got[plan[1, t]] = sums[...].astype(got.dtype)
            from_slot(t).start()

        return carry

    lax.fori_loop(0, tiles_here, many, 0)
    loss_out[0, 0] = jnp.max(loss_in[0:1, :])
    for t in range(tiles_here):
        from_zero(t).wait()
    save_emb.wait()


def place_tiles(plan, returned, grad_emb, loss, tiles_here):
    count, tile, width = returned.shape
    smem = pl.BlockSpec(memory_space=pltpu.SMEM)
    vmem = pl.BlockSpec(memory_space=pltpu.VMEM)
    hbm = pl.BlockSpec(memory_space=pltpu.HBM)
    dma = pltpu.SemaphoreType.DMA
    return pl.pallas_call(
        place_kernel,
        out_shape=(
            jax.ShapeDtypeStruct((tiles_here, tile, width), returned.dtype),
            jax.ShapeDtypeStruct(grad_emb.shape, grad_emb.dtype),
            jax.ShapeDtypeStruct((1, 1), jnp.float32),
        ),
        in_specs=[smem, hbm, hbm, vmem],
        out_specs=(hbm, hbm, smem),
        scratch_shapes=[
            pltpu.VMEM(returned.shape, returned.dtype),
            pltpu.VMEM(grad_emb.shape, grad_emb.dtype),
            pltpu.VMEM((tile, width), returned.dtype),
            pltpu.VMEM((tile, width), jnp.float32),
            dma,
            dma,
            dma((tiles_here,)),
        ],
        compiler_params=pltpu.CompilerParams(vmem_limit_bytes=VMEM_LIMIT),
    )(plan, returned, grad_emb, loss)


def main_kernel(
    coded,
    groups,
    dp_count,
    tiles_here,
    lists,
    labels,
    emb_hbm,
    table_hbm,
    grad_hbm,
    returned,
    loss_out,
    plan_out,
    table,
    emb,
    out_tiles,
    tiles,
    scores,
    partial,
    outgo,
    bound_in,
    bound_out,
    bound_own,
    bound_top,
    column,
    dz,
    piece,
    ret,
    grad,
    loss_acc,
    loss_mine,
    loss_plane,
    loss_sum,
    loss_z,
    select,
    my_slot,
    back,
    table_sem,
    emb_sem,
    grad_sem,
    tile_send,
    tile_recv,
    part_send,
    part_recv,
    bound_send,
    bound_recv,
    dz_send,
    dz_recv,
    ret_send,
    ret_recv,
    own_ret_sem,
    lp_send,
    lp_recv,
    lz_send,
    lz_recv,
    *incoming,
):
    me = lax.axis_index("proto")
    z = lax.axis_index("dp")
    rows, width = emb.shape
    list_len = lists.shape[1]
    parts, cols, _ = tiles.shape
    piece_rows = TILE // parts
    chunk = CHUNK[coded]
    half = rows // 2
    chunks = half // chunk
    dz_chunks = half // DZ_CHUNK
    ratio = DZ_CHUNK // chunk
    last = dp_count - 1
    block = 256
    inv_scale = 1.0 / math.sqrt(D)

    barrier = pltpu.get_barrier_semaphore()
    for k in range(1, groups):
        pl.semaphore_signal(
            barrier, inc=1, device_id={"proto": lax.rem(me + k, groups)}, device_id_type=MESH
        )
    for k in range(1, dp_count):
        pl.semaphore_signal(
            barrier, inc=1, device_id={"dp": lax.rem(z + k, dp_count)}, device_id_type=MESH
        )
    load_table = pltpu.make_async_copy(table_hbm, table, table_sem)
    load_table.start()
    load_emb = pltpu.make_async_copy(emb_hbm, emb, emb_sem)
    load_emb.start()

    base = me * tiles_here
    lane_one = lax.broadcasted_iota(jnp.int32, (1, 128), 1)
    count = jnp.zeros((1, 128), jnp.int32)
    first, second, held = count, count, count
    for b in range(groups):
        local = [lists[b, j] - base for j in range(list_len)]
        mine = [(t >= 0) & (t < tiles_here) for t in local]
        low, high = jnp.int32(0), jnp.int32(0)
        for j in range(list_len):
            high = jnp.where(mine[j], local[j], high)
            back_j = list_len - 1 - j
            low = jnp.where(mine[back_j], local[back_j], low)
        select[b * CAP] = low
        select[b * CAP + 1] = high
        listed = mine[0]
        for j in range(1, list_len):
            listed = listed | mine[j]
        for t, tile in enumerate((low, high)):
            slot = b * CAP + t
            tile = jnp.where(listed, tile, -1)
            hit = lane_one == tile
            count = count + jnp.where(hit, 1, 0)
            second = jnp.where(hit, first, second)
            first = jnp.where(hit, slot, first)
            held = jnp.where(lane_one == slot, tile, held)
    plan_out[0:1, :] = count
    plan_out[1:2, :] = first
    plan_out[2:3, :] = second
    plan_out[3:4, :] = held
    plan_out[4:8, :] = jnp.zeros((4, 128), jnp.int32)

    load_table.wait()
    for k in range(groups):
        to = lax.rem(me + k, groups)
        for t in range(CAP):
            slot = to * CAP + t
            for g in range(parts):
                tile = table[select[slot], g * piece_rows : (g + 1) * piece_rows, :]
                if k == 0:
                    incoming[g][slot] = tile
                else:
                    out_tiles[g, slot] = tile
    pl.semaphore_wait(barrier, groups + dp_count - 2)

    def tile_copy(g, k):
        to = lax.rem(me + k, groups)
        return pltpu.make_async_remote_copy(
            src_ref=out_tiles.at[g, pl.ds(to * CAP, CAP)],
            dst_ref=incoming[g].at[pl.ds(me * CAP, CAP)],
            send_sem=tile_send.at[g, k],
            recv_sem=tile_recv.at[g, k],
            device_id={"proto": to},
            device_id_type=MESH,
        )

    core = lax.rem(me, 2)
    for first in range(2):
        for g in range(parts):
            for a in range(groups // 2):
                k = lax.rem(2 * a + first - core + groups, groups)
                if a > 0:
                    tile_copy(g, k).start()
                else:

                    @pl.when(core != first)
                    def _():
                        tile_copy(g, k).start()

    ids = [lists[me, j] for j in range(list_len)]
    owner = [lax.div(t, jnp.int32(tiles_here)) for t in ids]
    flat = []
    for j in range(list_len):
        rank = jnp.int32(0)
        for i in range(j):
            rank = rank + jnp.where(owner[i] == owner[j], 1, 0)
        flat.append(owner[j] * CAP + rank)
        my_slot[j] = flat[j]
    for s in range(groups * CAP):
        at = jnp.int32(0)
        for j in range(1, list_len):
            at = jnp.where(flat[j] == s, j, at)
        back[s] = at
    lab = labels[...]
    lab_tile = lax.shift_right_logical(lab, 7)
    within = lax.bitwise_and(lab, TILE - 1)
    part_of = lax.shift_right_logical(within, int(math.log2(piece_rows)))
    where_to = part_of * cols + lax.bitwise_and(within, piece_rows - 1)
    for j in range(list_len):
        where_to = where_to + jnp.where(lab_tile == ids[j], j * piece_rows, 0)
    for i in range(rows // 128):
        column[i * 128 : (i + 1) * 128, :] = jnp.broadcast_to(where_to[i : i + 1, :], (128, 128)).T

    loss_acc[...] = jnp.zeros_like(loss_acc)
    bound_top[...] = jnp.zeros_like(bound_top)
    load_emb.wait()

    def tiles_in(g):
        for k in range(1, groups):
            tile_copy(g, k).wait_recv()
        for j in range(list_len):
            tiles[g, j * piece_rows : (j + 1) * piece_rows, :] = incoming[g][my_slot[j]]

    def rows_of(way, at):
        return pl.multiple_of((1 - way) * half + at, 32)

    def part_copy(way, g, c, first):
        here = pl.ds(pl.multiple_of(c * chunk, chunk), chunk)
        dst = partial.at[way, g, here]
        if coded:
            src = outgo.at[way, g, here]
        elif first:
            src = scores.at[g, pl.ds(rows_of(way, c * chunk), chunk)]
        else:
            src = dst
        return pltpu.make_async_remote_copy(
            src_ref=src,
            dst_ref=dst,
            send_sem=part_send.at[way, g, c],
            recv_sem=part_recv.at[way, g, c],
            device_id={"dp": jnp.clip(z + 1 - 2 * way, 0, last)},
            device_id_type=MESH,
        )

    def bound_copy(way, g):
        return pltpu.make_async_remote_copy(
            src_ref=bound_out.at[way, g],
            dst_ref=bound_in.at[way, g],
            send_sem=bound_send.at[way, g],
            recv_sem=bound_recv.at[way, g],
            device_id={"dp": jnp.clip(z + 1 - 2 * way, 0, last)},
            device_id_type=MESH,
        )

    def dz_copy(way, u):
        at = dz.at[u // dz_chunks, pl.ds(rows_of(way, lax.rem(u, dz_chunks) * DZ_CHUNK), DZ_CHUNK)]
        return pltpu.make_async_remote_copy(
            src_ref=at,
            dst_ref=at,
            send_sem=dz_send.at[way, u],
            recv_sem=dz_recv.at[way, u],
            device_id={"dp": jnp.clip(z - 1 + 2 * way, 0, last)},
            device_id_type=MESH,
        )

    def ret_copy(q, k):
        to = lax.rem(me + k, groups)
        return pltpu.make_async_remote_copy(
            src_ref=ret.at[q, pl.ds(to * CAP, CAP)],
            dst_ref=returned.at[pl.ds(me * CAP, CAP), pl.ds(pl.multiple_of(q * piece_rows, 16), piece_rows)],
            send_sem=ret_send.at[q, k],
            recv_sem=ret_recv.at[q, k],
            device_id={"proto": to},
            device_id_type=MESH,
        )

    def own_ret(q):
        return pltpu.make_async_copy(
            ret.at[q, pl.ds(me * CAP, CAP)],
            returned.at[pl.ds(me * CAP, CAP), pl.ds(pl.multiple_of(q * piece_rows, 16), piece_rows)],
            own_ret_sem.at[q],
        )

    lane = lax.broadcasted_iota(jnp.int32, (SOFT, cols), 1)

    def wide(x):
        return jnp.concatenate([x] * (cols // 128), axis=1) if cols > 128 else x

    def softmax_rows(i, start):
        at = pl.ds(pl.multiple_of(start + i * SOFT, SOFT), SOFT)
        target_at = wide(column[at, :])
        score = [scores[g, at, :] * inv_scale for g in range(parts)]
        top = score[0]
        for g in range(1, parts):
            top = jnp.maximum(top, score[g])
        top = jnp.max(top, axis=1, keepdims=True)
        expo = [jnp.exp(s - top) for s in score]
        total = expo[0]
        for g in range(1, parts):
            total = total + expo[g]
        total = jnp.sum(total, axis=1, keepdims=True)
        scale = 1.0 / total
        target = jnp.zeros((SOFT, cols), jnp.float32)
        for g in range(parts):
            onehot = lane + g * cols == target_at
            target = target + jnp.where(onehot, score[g], 0.0)
            dz[g, at, :] = (expo[g] * scale - jnp.where(onehot, 1.0, 0.0)).astype(dz.dtype)
        target = jnp.sum(target, axis=1, keepdims=True)
        loss_acc[...] += (top + jnp.log(total)) - target + jnp.zeros_like(loss_acc)
        return start

    def encode(way, g, c, value):
        here = pl.ds(pl.multiple_of(c * chunk, chunk), chunk)
        gain = wide(CODE_MAX / bound_out[way, g, 0:1, :])
        code = (value * gain + ROUND) - ROUND
        outgo[way, g, here, :] = code.astype(jnp.int32).astype(outgo.dtype)

    def decode(way, g, c):
        here = pl.ds(pl.multiple_of(c * chunk, chunk), chunk)
        if not coded:
            return partial[way, g, here, :]
        gain = wide(bound_in[way, g, 0:1, :] * (1.0 / CODE_MAX))
        return partial[way, g, here, :].astype(jnp.int32).astype(jnp.float32) * gain

    def new_block(g):
        biggest = []
        for r in range(rows // block):
            these = slice(r * block, (r + 1) * block)
            value = lax.dot_general(
                emb[these, :], tiles[g], (((1,), (1,)), ((), ())), preferred_element_type=jnp.float32
            )
            scores[g, these, :] = value
            if coded:
                biggest.append(jnp.max(jnp.abs(value), axis=0, keepdims=True))
        if coded:
            per_way = len(biggest) // 2
            for way in range(2):
                some = biggest[(1 - way) * per_way : (2 - way) * per_way]
                top = some[0]
                for x in some[1:]:
                    top = jnp.maximum(top, x)
                top = jnp.max(top, axis=1, keepdims=True)
                bound_own[way, g] = jnp.broadcast_to(jnp.maximum(top, 1e-20), (8, 128))

    def new_bound(way, g, pos):
        @pl.when(pos == 0)
        def _():
            bound_out[way, g] = bound_own[way, g]

        @pl.when(pos > 0)
        def _():
            bound_copy(way, g).wait_recv()
            bound_out[way, g] = bound_in[way, g] + bound_own[way, g]

        @pl.when(pos < last)
        def _():
            bound_copy(way, g).start()
            bound_top[...] = jnp.maximum(bound_top[...], bound_out[way, g])

    dz_start = (parts - 1) * chunks + LAG * last
    tail_start = ratio * dz_chunks
    ret_start = -(-(dz_start + tail_start + DZ_LAG * last) // dz_chunks) * dz_chunks

    def send_pieces(q):
        out = lax.dot_general(
            dz[q], emb[...], (((0,), (0,)), ((), ())), preferred_element_type=jnp.float32
        ).astype(piece.dtype)
        for j in range(list_len):
            piece[j] = out[j * piece_rows : (j + 1) * piece_rows, :]
        for k in range(1, groups):
            to = lax.rem(me + k, groups)
            for t in range(CAP):
                ret[q, to * CAP + t] = piece[back[to * CAP + t]]
            ret_copy(q, k).start()
        for t in range(CAP):
            ret[q, me * CAP + t] = piece[back[me * CAP + t]]
        own_ret(q).start()

    def lp_copy(k):
        return pltpu.make_async_remote_copy(
            src_ref=loss_mine,
            dst_ref=loss_plane.at[me],
            send_sem=lp_send.at[k],
            recv_sem=lp_recv.at[k],
            device_id={"proto": lax.rem(me + k, groups)},
            device_id_type=MESH,
        )

    def lz_copy(k):
        return pltpu.make_async_remote_copy(
            src_ref=loss_sum,
            dst_ref=loss_z.at[z],
            send_sem=lz_send.at[k],
            recv_sem=lz_recv.at[k],
            device_id={"dp": lax.rem(z + k, dp_count)},
            device_id_type=MESH,
        )

    def loss_begin():
        mine = jnp.broadcast_to(jnp.sum(loss_acc[...], axis=0, keepdims=True), (8, 128))
        too_big = jnp.where(bound_top[...] * inv_scale > BOUND, 1.0, 0.0)
        loss_mine[...] = jnp.where(lax.broadcasted_iota(jnp.int32, (8, 128), 0) < 4, mine, too_big)
        loss_plane[me] = loss_mine[...]
        for k in range(1, groups):
            lp_copy(k).start()

    def loss_middle():
        for k in range(1, groups):
            lp_copy(k).wait()
        plane = loss_plane[0]
        for k in range(1, groups):
            plane = plane + loss_plane[k]
        loss_sum[...] = plane
        loss_z[z] = plane
        for k in range(1, dp_count):
            lz_copy(k).start()

    def loss_end():
        for k in range(1, dp_count):
            lz_copy(k).wait()
        whole = loss_z[0]
        for k in range(1, dp_count):
            whole = whole + loss_z[k]
        loss_out[...] = whole * (1.0 / (rows * groups))

    def events(at):
        @pl.when((at < parts * chunks) & (lax.rem(at, chunks) == 0))
        def _():
            for g in range(parts):

                @pl.when(at == g * chunks)
                def _():
                    tiles_in(g)

            new_block(at // chunks)

        @pl.when(at == ret_start)
        def _():
            loss_begin()

        @pl.when(at >= ret_start)
        def _():
            send_pieces((at - ret_start) // dz_chunks)

    def step(i, at):
        way = lax.rem(i, 2)
        s = at + i // 2
        pos = jnp.where(way == 0, z, last - z)
        turn = s - LAG * pos

        @pl.when((turn >= 0) & (turn < parts * chunks))
        def _():
            g = turn // chunks
            c = lax.rem(turn, chunks)

            if coded:

                @pl.when(c == 0)
                def _():
                    new_bound(way, g, pos)

            at = pl.ds(rows_of(way, c * chunk), chunk)

            @pl.when(pos == 0)
            def _():
                if coded:
                    encode(way, g, c, scores[g, at, :])
                part_copy(way, g, c, True).start()

            @pl.when((pos > 0) & (pos < last))
            def _():
                part_copy(way, g, c, False).wait_recv()
                value = decode(way, g, c) + scores[g, at, :]
                if coded:
                    encode(way, g, c, value)
                else:
                    partial[way, g, pl.ds(pl.multiple_of(c * chunk, chunk), chunk), :] = value
                part_copy(way, g, c, False).start()

            @pl.when(pos == last)
            def _():
                part_copy(way, g, c, False).wait_recv()
                scores[g, at, :] += decode(way, g, c)

            @pl.when((pos == last) & (g == parts - 1))
            def _():
                lax.fori_loop(0, chunk // SOFT, softmax_rows, rows_of(way, c * chunk))

        d = s - dz_start - DZ_LAG * (last - pos)
        u = jnp.where(d < tail_start, d // ratio, d - tail_start + dz_chunks)
        now = (d >= 0) & (u < parts * dz_chunks)
        now = now & ((d >= tail_start) | (lax.rem(d + ratio, ratio) == ratio - 1))

        @pl.when(now & (pos < last))
        def _():
            dz_copy(way, u).wait_recv()

        @pl.when(now & (pos > 0))
        def _():
            dz_copy(way, u).start()

        return at

    def stage(j, carry):
        at = j * dz_chunks
        events(at)
        lax.fori_loop(0, 2 * dz_chunks, step, at)
        return carry

    lax.fori_loop(0, ret_start // dz_chunks + parts - 1, stage, 0)
    events(jnp.int32(ret_start + (parts - 1) * dz_chunks))
    loss_middle()

    def save_grad(i):
        at = pl.ds(pl.multiple_of(i * block, block), block)
        return pltpu.make_async_copy(grad.at[at], grad_hbm.at[at], grad_sem.at[i])

    def grad_block(i, carry):
        at = pl.ds(pl.multiple_of(i * block, block), block)
        total = jnp.dot(dz[0, at, :], tiles[0], preferred_element_type=jnp.float32)
        for g in range(1, parts):
            total = total + jnp.dot(dz[g, at, :], tiles[g], preferred_element_type=jnp.float32)
        grad[at, :] = total.astype(grad.dtype)
        save_grad(i).start()
        return carry

    lax.fori_loop(0, rows // block, grad_block, 0)

    loss_end()

    def drain_parts(i, carry):
        way = lax.rem(i, 2)
        turn = i // 2

        @pl.when(jnp.where(way == 0, z, last - z) < last)
        def _():
            part_copy(way, turn // chunks, lax.rem(turn, chunks), False).wait_send()

        return carry

    lax.fori_loop(0, 2 * parts * chunks, drain_parts, 0)

    def drain_dz(i, carry):
        way = lax.rem(i, 2)

        @pl.when(jnp.where(way == 0, z, last - z) > 0)
        def _():
            dz_copy(way, i // 2).wait_send()

        return carry

    lax.fori_loop(0, 2 * parts * dz_chunks, drain_dz, 0)
    if coded:

        def drain_bounds(i, carry):
            way = lax.rem(i, 2)

            @pl.when(jnp.where(way == 0, z, last - z) < last)
            def _():
                bound_copy(way, i // 2).wait_send()

            return carry

        lax.fori_loop(0, 2 * parts, drain_bounds, 0)
    for g in range(parts):
        for k in range(1, groups):
            tile_copy(g, k).wait_send()
    for i in range(rows // block):
        save_grad(i).wait()

    def drain_ret(q, carry):
        own_ret(q).wait()
        for k in range(1, groups):
            ret_copy(q, k).wait()
        return carry

    lax.fori_loop(0, parts, drain_ret, 0)


def run_main(coded, lists, labels, embeddings, table):
    block_rows, width = embeddings.shape
    list_len = lists.shape[1]
    tiles_here = table.shape[0] // TILE
    groups = lax.axis_size("proto")
    dp_count = lax.axis_size("dp")
    slots = groups * CAP
    cols = list_len * TILE // PARTS
    piece_rows = TILE // PARTS
    half = block_rows // 2
    chunks = half // CHUNK[coded]
    dz_chunks = half // DZ_CHUNK
    bf16, f32, i32 = jnp.bfloat16, jnp.float32, jnp.int32
    dma = pltpu.SemaphoreType.DMA
    vmem = pl.BlockSpec(memory_space=pltpu.VMEM)
    smem = pl.BlockSpec(memory_space=pltpu.SMEM)
    hbm = pl.BlockSpec(memory_space=pltpu.HBM)
    wire = (2, PARTS, half, cols)
    small = (2, PARTS, 8, 128)
    return pl.pallas_call(
        functools.partial(main_kernel, coded, groups, dp_count, tiles_here),
        out_shape=(
            jax.ShapeDtypeStruct((block_rows, width), bf16),
            jax.ShapeDtypeStruct((slots, TILE, width), bf16),
            jax.ShapeDtypeStruct((8, 128), f32),
            jax.ShapeDtypeStruct((8, 128), i32),
        ),
        in_specs=[smem, vmem, hbm, hbm],
        out_specs=(hbm, hbm, vmem, vmem),
        scratch_shapes=[
            pltpu.VMEM((tiles_here, TILE, width), bf16),
            pltpu.VMEM((block_rows, width), bf16),
            pltpu.VMEM((PARTS, slots, piece_rows, width), bf16),
            pltpu.VMEM((PARTS, cols, width), bf16),
            pltpu.VMEM((PARTS, block_rows, cols), f32),
            pltpu.VMEM(wire, jnp.int16 if coded else f32),
            pltpu.VMEM(wire if coded else (2, PARTS, 16, cols), jnp.int16),
            pltpu.VMEM(small, f32),
            pltpu.VMEM(small, f32),
            pltpu.VMEM(small, f32),
            pltpu.VMEM((8, 128), f32),
            pltpu.VMEM((block_rows, 128), i32),
            pltpu.VMEM((PARTS, block_rows, cols), bf16),
            pltpu.VMEM((list_len, piece_rows, width), bf16),
            pltpu.VMEM((PARTS, slots, piece_rows, width), bf16),
            pltpu.VMEM((block_rows, width), bf16),
            pltpu.VMEM((SOFT, 128), f32),
            pltpu.VMEM((8, 128), f32),
            pltpu.VMEM((groups, 8, 128), f32),
            pltpu.VMEM((8, 128), f32),
            pltpu.VMEM((dp_count, 8, 128), f32),
            pltpu.SMEM((slots,), i32),
            pltpu.SMEM((list_len,), i32),
            pltpu.SMEM((slots,), i32),
            dma,
            dma,
            dma((block_rows // 256,)),
            dma((PARTS, groups)),
            dma((PARTS, groups)),
            dma((2, PARTS, chunks)),
            dma((2, PARTS, chunks)),
            dma((2, PARTS)),
            dma((2, PARTS)),
            dma((2, PARTS * dz_chunks)),
            dma((2, PARTS * dz_chunks)),
            dma((PARTS, groups)),
            dma((PARTS, groups)),
            dma((PARTS,)),
            dma((groups,)),
            dma((groups,)),
            dma((dp_count,)),
            dma((dp_count,)),
        ]
        + [pltpu.VMEM((slots, piece_rows, width), bf16)] * PARTS,
        compiler_params=pltpu.CompilerParams(
            collective_id=int(coded), has_side_effects=True, vmem_limit_bytes=VMEM_LIMIT
        ),
    )(lists, labels.reshape(block_rows // 128, 128), embeddings, table.reshape(tiles_here, TILE, width))


def fused_body(embeddings, table, tile_lists, labels):
    tiles_here = table.shape[0] // TILE
    inputs = (tile_lists, labels, embeddings, table)

    def finish(grad_emb, returned, loss, plan):
        return place_tiles(plan, returned, grad_emb, loss, tiles_here)

    if GUARD == 0:
        grad_table, grad_emb, loss = finish(*run_main(True, *inputs))
    else:
        coded = run_main(True, *inputs)
        grad_table, grad_emb, loss = lax.cond(
            coded[2][7, 0] > 0.0,
            lambda coded, inputs: finish(*run_main(False, *inputs)),
            lambda coded, inputs: finish(*coded),
            coded,
            inputs,
        )
    return (loss.reshape(()), grad_emb, grad_table.reshape(table.shape))


def any_body(embeddings, table, tile_lists, labels):
    block_rows, width = embeddings.shape
    cols = tile_lists.shape[1] * TILE
    need = block_rows * cols * (4 + 4 + 2 + 2) + 2 * table.shape[0] * width * 2
    if need + 8 * 2**20 <= VMEM_LIMIT and block_rows % 1024 == 0:
        return fused_body(embeddings, table, tile_lists, labels)
    return body(embeddings, table, tile_lists, labels)


def solution(mesh):
    placed = (P("proto", "dp"), P("proto", "dp"), P(), P("proto"))
    return jax.shard_map(
        any_body,
        mesh=mesh,
        in_specs=placed,
        out_specs=(P(), P("proto", "dp"), P("proto", "dp")),
        check_vma=False,
    )
```

```python
import functools
import math

import jax
import jax.numpy as jnp
from jax import lax
from jax.experimental import pallas as pl
from jax.experimental.pallas import tpu as pltpu
from jax.sharding import PartitionSpec as P

D = 2560
TILE = 128
CAP = 2
PARTS = 8
CHUNK = {False: 64, True: 256}
DZ_CHUNK = 256
LAG_FIRST = 4
LAG = 4
LAG_LAST = 4
DZ_FIRST = 1
DZ_LAG = 4
DZ_LAST = 1
CODE_MAX = 32766.0
GUARD = 1
BOUND = 48.0
SOFT = 32
ROUND = 12582912.0
VMEM_LIMIT = 56 * 2**20
MESH = pl.DeviceIdType.MESH


def slot_plan(ids, tiles_here):
    owners = ids // tiles_here
    local = ids % tiles_here
    count = ids.shape[-1]
    before = jnp.arange(count)[:, None] > jnp.arange(count)[None, :]
    earlier = (owners[..., :, None] == owners[..., None, :]) & before
    rank = jnp.sum(earlier.astype(jnp.int32), axis=-1)
    return (owners, local, rank)


def softmax_terms(scores, ids, lab, list_len):
    hit = (ids[None, :] == (lab // TILE)[:, None]).astype(jnp.int32)
    column = (
        jnp.sum(hit * (jnp.arange(list_len, dtype=jnp.int32) * TILE)[None, :], axis=1) + lab % TILE
    )
    onehot = (jnp.arange(list_len * TILE, dtype=jnp.int32)[None, :] == column[:, None]).astype(
        jnp.float32
    )
    top = jnp.max(scores, axis=1, keepdims=True)
    expo = jnp.exp(scores - top)
    total = jnp.sum(expo, axis=1, keepdims=True)
    lse = top[:, 0] + jnp.log(total[:, 0])
    target = jnp.sum(scores * onehot, axis=1)
    dz_rows = (expo / total - onehot).astype(jnp.bfloat16)
    return (jnp.sum(lse - target), dz_rows)


def body(embeddings, table, tile_lists, labels):
    block_rows, width = embeddings.shape
    list_len = tile_lists.shape[1]
    tiles_here = table.shape[0] // TILE
    groups = lax.axis_size("proto")
    dp_count = lax.axis_size("dp")
    rows_dev = block_rows // dp_count
    total_rows = block_rows * groups
    me = lax.axis_index("proto")
    part = lax.axis_index("dp")
    inv_scale = 1.0 / math.sqrt(D)
    owners, local, rank = slot_plan(tile_lists, tiles_here)
    match = (owners == me)[:, :, None] & (
        rank[:, :, None] == jnp.arange(CAP, dtype=jnp.int32)[None, None, :]
    )
    select = jnp.sum(match.astype(jnp.int32) * local[:, :, None], axis=1)
    shaped_table = table.reshape(tiles_here, TILE, width)
    outgoing = pack_tiles(shaped_table, select.reshape(-1)).reshape(groups, CAP, TILE, width)
    incoming = lax.all_to_all(outgoing, "proto", split_axis=0, concat_axis=0, tiled=True)
    my_ids = lax.dynamic_index_in_dim(tile_lists, me, 0, keepdims=False)
    my_owner = lax.dynamic_index_in_dim(owners, me, 0, keepdims=False)
    my_rank = lax.dynamic_index_in_dim(rank, me, 0, keepdims=False)
    flat_slot = my_owner * CAP + my_rank
    tiles = pack_tiles(incoming.reshape(groups * CAP, TILE, width), flat_slot).reshape(
        list_len * TILE, width
    )
    scores = (
        lax.psum_scatter(
            lax.dot_general(
                embeddings, tiles, (((1,), (1,)), ((), ())), preferred_element_type=jnp.float32
            ),
            "dp",
            scatter_dimension=0,
            tiled=True,
        )
        * inv_scale
    )
    my_labels = lax.dynamic_slice_in_dim(labels, part * rows_dev, rows_dev, 0)
    loss_part, dz_rows = softmax_terms(scores, my_ids, my_labels, list_len)
    dz_block = lax.all_gather(dz_rows, "dp", axis=0, tiled=True)
    loss = lax.psum(loss_part, ("dp", "proto")) / total_rows
    grad_emb = jnp.dot(dz_block, tiles, preferred_element_type=jnp.float32).astype(jnp.bfloat16)
    piece = lax.dot_general(
        dz_block, embeddings, (((0,), (0,)), ((), ())), preferred_element_type=jnp.float32
    ).astype(jnp.bfloat16)
    returning = (
        jnp.zeros((groups * CAP, TILE, width), jnp.bfloat16)
        .at[flat_slot]
        .set(piece.reshape(list_len, TILE, width))
    )
    returned = lax.all_to_all(
        returning.reshape(groups, CAP, TILE, width),
        "proto",
        split_axis=0,
        concat_axis=0,
        tiled=True,
    )
    accum = (
        jnp.zeros((tiles_here, TILE, width), jnp.float32)
        .at[select.reshape(-1)]
        .add(returned.reshape(groups * CAP, TILE, width))
    )
    grad_table = accum.reshape(tiles_here * TILE, width).astype(jnp.bfloat16)
    return (loss, grad_emb, grad_table)


def pack_kernel(pick_ref, table_ref, out_ref, sems):
    count = out_ref.shape[0]

    def copy(slot):
        return pltpu.make_async_copy(
            table_ref.at[pick_ref[slot]], out_ref.at[slot], sems.at[slot]
        )

    for slot in range(count):
        copy(slot).start()
    for slot in range(count):
        copy(slot).wait()


def pack_tiles(shaped_table, pick):
    count = pick.shape[0]
    _, tile, width = shaped_table.shape
    return pl.pallas_call(
        pack_kernel,
        out_shape=jax.ShapeDtypeStruct((count, tile, width), shaped_table.dtype),
        grid_spec=pltpu.PrefetchScalarGridSpec(
            num_scalar_prefetch=1,
            grid=(1,),
            in_specs=[pl.BlockSpec(memory_space=pl.ANY)],
            out_specs=pl.BlockSpec(memory_space=pltpu.VMEM),
            scratch_shapes=[pltpu.SemaphoreType.DMA((count,))],
        ),
        compiler_params=pltpu.CompilerParams(vmem_limit_bytes=32 * 2**20),
    )(pick, shaped_table)


def place_kernel(plan, returned, emb_in, loss_in, table_out, emb_out, loss_out, got, emb, zero, sums, in_sem, emb_sem, out_sem):
    tiles_here = table_out.shape[0]
    count = returned.shape[0]
    load = pltpu.make_async_copy(returned, got, in_sem)
    load.start()
    load_emb = pltpu.make_async_copy(emb_in, emb, emb_sem)
    load_emb.start()
    zero[...] = jnp.zeros_like(zero)

    def from_zero(t):
        return pltpu.make_async_copy(zero, table_out.at[t], out_sem.at[t])

    def from_slot(t):
        return pltpu.make_async_copy(got.at[plan[1, t]], table_out.at[t], out_sem.at[t])

    for t in range(tiles_here):

        @pl.when(plan[0, t] == 0)
        def _():
            from_zero(t).start()

    load_emb.wait()
    save_emb = pltpu.make_async_copy(emb, emb_out, emb_sem)
    save_emb.start()
    load.wait()
    for t in range(tiles_here):

        @pl.when(plan[0, t] == 1)
        def _():
            from_slot(t).start()

    def many(t, carry):
        @pl.when(plan[0, t] == 2)
        def _():
            sums[...] = got[plan[1, t]].astype(jnp.float32) + got[plan[2, t]].astype(jnp.float32)

        @pl.when(plan[0, t] > 2)
        def _():
            sums[...] = jnp.zeros_like(sums)

            def add(slot, carry):
                @pl.when(plan[3, slot] == t)
                def _():
                    sums[...] += got[slot].astype(jnp.float32)

                return carry

            lax.fori_loop(0, count, add, 0)

        @pl.when(plan[0, t] > 1)
        def _():
            got[plan[1, t]] = sums[...].astype(got.dtype)
            from_slot(t).start()

        return carry

    lax.fori_loop(0, tiles_here, many, 0)
    loss_out[0, 0] = jnp.max(loss_in[0:1, :])
    for t in range(tiles_here):
        from_zero(t).wait()
    save_emb.wait()


def place_tiles(plan, returned, grad_emb, loss, tiles_here):
    count, tile, width = returned.shape
    smem = pl.BlockSpec(memory_space=pltpu.SMEM)
    vmem = pl.BlockSpec(memory_space=pltpu.VMEM)
    hbm = pl.BlockSpec(memory_space=pltpu.HBM)
    dma = pltpu.SemaphoreType.DMA
    return pl.pallas_call(
        place_kernel,
        out_shape=(
            jax.ShapeDtypeStruct((tiles_here, tile, width), returned.dtype),
            jax.ShapeDtypeStruct(grad_emb.shape, grad_emb.dtype),
            jax.ShapeDtypeStruct((1, 1), jnp.float32),
        ),
        in_specs=[smem, hbm, hbm, vmem],
        out_specs=(hbm, hbm, smem),
        scratch_shapes=[
            pltpu.VMEM(returned.shape, returned.dtype),
            pltpu.VMEM(grad_emb.shape, grad_emb.dtype),
            pltpu.VMEM((tile, width), returned.dtype),
            pltpu.VMEM((tile, width), jnp.float32),
            dma,
            dma,
            dma((tiles_here,)),
        ],
        compiler_params=pltpu.CompilerParams(vmem_limit_bytes=VMEM_LIMIT),
    )(plan, returned, grad_emb, loss)


def main_kernel(
    coded,
    groups,
    dp_count,
    tiles_here,
    lists,
    labels,
    emb_hbm,
    table_hbm,
    grad_hbm,
    returned,
    loss_out,
    plan_out,
    table,
    emb,
    out_tiles,
    tiles,
    scores,
    partial,
    outgo,
    bound_in,
    bound_out,
    bound_own,
    bound_top,
    column,
    dz,
    piece,
    ret,
    grad,
    loss_acc,
    loss_mine,
    loss_plane,
    loss_sum,
    loss_z,
    select,
    my_slot,
    back,
    table_sem,
    emb_sem,
    grad_sem,
    tile_send,
    tile_recv,
    part_send,
    part_recv,
    bound_send,
    bound_recv,
    dz_send,
    dz_recv,
    ret_send,
    ret_recv,
    own_ret_sem,
    lp_send,
    lp_recv,
    lz_send,
    lz_recv,
    *incoming,
):
    me = lax.axis_index("proto")
    z = lax.axis_index("dp")
    rows, width = emb.shape
    list_len = lists.shape[1]
    parts, cols, _ = tiles.shape
    piece_rows = TILE // parts
    chunk = CHUNK[coded]
    half = rows // 2
    chunks = half // chunk
    dz_chunks = half // DZ_CHUNK
    ratio = DZ_CHUNK // chunk
    last = dp_count - 1
    block = 256
    inv_scale = 1.0 / math.sqrt(D)

    barrier = pltpu.get_barrier_semaphore()
    for k in range(1, groups):
        pl.semaphore_signal(
            barrier, inc=1, device_id={"proto": lax.rem(me + k, groups)}, device_id_type=MESH
        )
    for k in range(1, dp_count):
        pl.semaphore_signal(
            barrier, inc=1, device_id={"dp": lax.rem(z + k, dp_count)}, device_id_type=MESH
        )
    load_table = pltpu.make_async_copy(table_hbm, table, table_sem)
    load_table.start()
    load_emb = pltpu.make_async_copy(emb_hbm, emb, emb_sem)
    load_emb.start()

    base = me * tiles_here
    lane_one = lax.broadcasted_iota(jnp.int32, (1, 128), 1)
    count = jnp.zeros((1, 128), jnp.int32)
    first, second, held = count, count, count
    for b in range(groups):
        local = [lists[b, j] - base for j in range(list_len)]
        mine = [(t >= 0) & (t < tiles_here) for t in local]
        low, high = jnp.int32(0), jnp.int32(0)
        for j in range(list_len):
            high = jnp.where(mine[j], local[j], high)
            back_j = list_len - 1 - j
            low = jnp.where(mine[back_j], local[back_j], low)
        select[b * CAP] = low
        select[b * CAP + 1] = high
        listed = mine[0]
        for j in range(1, list_len):
            listed = listed | mine[j]
        for t, tile in enumerate((low, high)):
            slot = b * CAP + t
            tile = jnp.where(listed, tile, -1)
            hit = lane_one == tile
            count = count + jnp.where(hit, 1, 0)
            second = jnp.where(hit, first, second)
            first = jnp.where(hit, slot, first)
            held = jnp.where(lane_one == slot, tile, held)
    plan_out[0:1, :] = count
    plan_out[1:2, :] = first
    plan_out[2:3, :] = second
    plan_out[3:4, :] = held
    plan_out[4:8, :] = jnp.zeros((4, 128), jnp.int32)

    load_table.wait()
    for k in range(groups):
        to = lax.rem(me + k, groups)
        for t in range(CAP):
            slot = to * CAP + t
            for g in range(parts):
                tile = table[select[slot], g * piece_rows : (g + 1) * piece_rows, :]
                if k == 0:
                    incoming[g][slot] = tile
                else:
                    out_tiles[g, slot] = tile
    pl.semaphore_wait(barrier, groups + dp_count - 2)

    def tile_copy(g, k):
        to = lax.rem(me + k, groups)
        return pltpu.make_async_remote_copy(
            src_ref=out_tiles.at[g, pl.ds(to * CAP, CAP)],
            dst_ref=incoming[g].at[pl.ds(me * CAP, CAP)],
            send_sem=tile_send.at[g, k],
            recv_sem=tile_recv.at[g, k],
            device_id={"proto": to},
            device_id_type=MESH,
        )

    core = lax.rem(me, 2)
    for first in range(2):
        for g in range(parts):
            for a in range(groups // 2):
                k = lax.rem(2 * a + first - core + groups, groups)
                if a > 0:
                    tile_copy(g, k).start()
                else:

                    @pl.when(core != first)
                    def _():
                        tile_copy(g, k).start()

    ids = [lists[me, j] for j in range(list_len)]
    owner = [lax.div(t, jnp.int32(tiles_here)) for t in ids]
    flat = []
    for j in range(list_len):
        rank = jnp.int32(0)
        for i in range(j):
            rank = rank + jnp.where(owner[i] == owner[j], 1, 0)
        flat.append(owner[j] * CAP + rank)
        my_slot[j] = flat[j]
    for s in range(groups * CAP):
        at = jnp.int32(0)
        for j in range(1, list_len):
            at = jnp.where(flat[j] == s, j, at)
        back[s] = at
    lab = labels[...]
    lab_tile = lax.shift_right_logical(lab, 7)
    within = lax.bitwise_and(lab, TILE - 1)
    part_of = lax.shift_right_logical(within, int(math.log2(piece_rows)))
    where_to = part_of * cols + lax.bitwise_and(within, piece_rows - 1)
    for j in range(list_len):
        where_to = where_to + jnp.where(lab_tile == ids[j], j * piece_rows, 0)
    for i in range(rows // 128):
        column[i * 128 : (i + 1) * 128, :] = jnp.broadcast_to(where_to[i : i + 1, :], (128, 128)).T

    loss_acc[...] = jnp.zeros_like(loss_acc)
    bound_top[...] = jnp.zeros_like(bound_top)
    load_emb.wait()

    def tiles_in(g):
        for k in range(1, groups):
            tile_copy(g, k).wait_recv()
        for j in range(list_len):
            tiles[g, j * piece_rows : (j + 1) * piece_rows, :] = incoming[g][my_slot[j]]

    def rows_of(way, at):
        return pl.multiple_of((1 - way) * half + at, 32)

    def part_copy(way, g, c, first):
        here = pl.ds(pl.multiple_of(c * chunk, chunk), chunk)
        dst = partial.at[way, g, here]
        if coded:
            src = outgo.at[way, g, here]
        elif first:
            src = scores.at[g, pl.ds(rows_of(way, c * chunk), chunk)]
        else:
            src = dst
        return pltpu.make_async_remote_copy(
            src_ref=src,
            dst_ref=dst,
            send_sem=part_send.at[way, g, c],
            recv_sem=part_recv.at[way, g, c],
            device_id={"dp": jnp.clip(z + 1 - 2 * way, 0, last)},
            device_id_type=MESH,
        )

    def bound_copy(way, g):
        return pltpu.make_async_remote_copy(
            src_ref=bound_out.at[way, g],
            dst_ref=bound_in.at[way, g],
            send_sem=bound_send.at[way, g],
            recv_sem=bound_recv.at[way, g],
            device_id={"dp": jnp.clip(z + 1 - 2 * way, 0, last)},
            device_id_type=MESH,
        )

    def dz_copy(way, u):
        at = dz.at[u // dz_chunks, pl.ds(rows_of(way, lax.rem(u, dz_chunks) * DZ_CHUNK), DZ_CHUNK)]
        return pltpu.make_async_remote_copy(
            src_ref=at,
            dst_ref=at,
            send_sem=dz_send.at[way, u],
            recv_sem=dz_recv.at[way, u],
            device_id={"dp": jnp.clip(z - 1 + 2 * way, 0, last)},
            device_id_type=MESH,
        )

    def ret_copy(q, k):
        to = lax.rem(me + k, groups)
        return pltpu.make_async_remote_copy(
            src_ref=ret.at[q, pl.ds(to * CAP, CAP)],
            dst_ref=returned.at[pl.ds(me * CAP, CAP), pl.ds(pl.multiple_of(q * piece_rows, 16), piece_rows)],
            send_sem=ret_send.at[q, k],
            recv_sem=ret_recv.at[q, k],
            device_id={"proto": to},
            device_id_type=MESH,
        )

    def own_ret(q):
        return pltpu.make_async_copy(
            ret.at[q, pl.ds(me * CAP, CAP)],
            returned.at[pl.ds(me * CAP, CAP), pl.ds(pl.multiple_of(q * piece_rows, 16), piece_rows)],
            own_ret_sem.at[q],
        )

    lane = lax.broadcasted_iota(jnp.int32, (SOFT, cols), 1)

    def wide(x):
        return jnp.concatenate([x] * (cols // 128), axis=1) if cols > 128 else x

    def softmax_rows(i, start):
        at = pl.ds(pl.multiple_of(start + i * SOFT, SOFT), SOFT)
        target_at = wide(column[at, :])
        score = [scores[g, at, :] * inv_scale for g in range(parts)]
        top = score[0]
        for g in range(1, parts):
            top = jnp.maximum(top, score[g])
        top = jnp.max(top, axis=1, keepdims=True)
        expo = [jnp.exp(s - top) for s in score]
        total = expo[0]
        for g in range(1, parts):
            total = total + expo[g]
        total = jnp.sum(total, axis=1, keepdims=True)
        scale = 1.0 / total
        target = jnp.zeros((SOFT, cols), jnp.float32)
        for g in range(parts):
            onehot = lane + g * cols == target_at
            target = target + jnp.where(onehot, score[g], 0.0)
            dz[g, at, :] = (expo[g] * scale - jnp.where(onehot, 1.0, 0.0)).astype(dz.dtype)
        target = jnp.sum(target, axis=1, keepdims=True)
        loss_acc[...] += (top + jnp.log(total)) - target + jnp.zeros_like(loss_acc)
        return start

    def encode(way, g, c, value):
        here = pl.ds(pl.multiple_of(c * chunk, chunk), chunk)
        gain = wide(CODE_MAX / bound_out[way, g, 0:1, :])
        code = (value * gain + ROUND) - ROUND
        outgo[way, g, here, :] = code.astype(jnp.int32).astype(outgo.dtype)

    def decode(way, g, c):
        here = pl.ds(pl.multiple_of(c * chunk, chunk), chunk)
        if not coded:
            return partial[way, g, here, :]
        gain = wide(bound_in[way, g, 0:1, :] * (1.0 / CODE_MAX))
        return partial[way, g, here, :].astype(jnp.int32).astype(jnp.float32) * gain

    def new_block(g):
        biggest = []
        for r in range(rows // block):
            these = slice(r * block, (r + 1) * block)
            value = lax.dot_general(
                emb[these, :], tiles[g], (((1,), (1,)), ((), ())), preferred_element_type=jnp.float32
            )
            scores[g, these, :] = value
            if coded:
                biggest.append(jnp.max(jnp.abs(value), axis=0, keepdims=True))
        if coded:
            per_way = len(biggest) // 2
            for way in range(2):
                some = biggest[(1 - way) * per_way : (2 - way) * per_way]
                top = some[0]
                for x in some[1:]:
                    top = jnp.maximum(top, x)
                top = jnp.max(top, axis=1, keepdims=True)
                bound_own[way, g] = jnp.broadcast_to(jnp.maximum(top, 1e-20), (8, 128))

    def new_bound(way, g, pos):
        @pl.when(pos == 0)
        def _():
            bound_out[way, g] = bound_own[way, g]

        @pl.when(pos > 0)
        def _():
            bound_copy(way, g).wait_recv()
            bound_out[way, g] = bound_in[way, g] + bound_own[way, g]

        @pl.when(pos < last)
        def _():
            bound_copy(way, g).start()
            bound_top[...] = jnp.maximum(bound_top[...], bound_out[way, g])

    def lag(hops, first, middle, final):
        between = jnp.maximum(jnp.minimum(hops - 1, last - 2), 0) * middle
        return jnp.where(hops == 0, 0, first + between + jnp.where(hops == last, final, 0))

    part_total = LAG_FIRST + max(last - 2, 0) * LAG + LAG_LAST
    dz_total = DZ_FIRST + max(last - 2, 0) * DZ_LAG + DZ_LAST
    dz_start = (parts - 1) * chunks + part_total
    tail_start = ratio * dz_chunks
    ret_start = -(-(dz_start + tail_start + dz_total) // dz_chunks) * dz_chunks

    def send_pieces(q):
        out = lax.dot_general(
            dz[q], emb[...], (((0,), (0,)), ((), ())), preferred_element_type=jnp.float32
        ).astype(piece.dtype)
        for j in range(list_len):
            piece[j] = out[j * piece_rows : (j + 1) * piece_rows, :]
        for k in range(1, groups):
            to = lax.rem(me + k, groups)
            for t in range(CAP):
                ret[q, to * CAP + t] = piece[back[to * CAP + t]]
            ret_copy(q, k).start()
        for t in range(CAP):
            ret[q, me * CAP + t] = piece[back[me * CAP + t]]
        own_ret(q).start()

    def lp_copy(k):
        return pltpu.make_async_remote_copy(
            src_ref=loss_mine,
            dst_ref=loss_plane.at[me],
            send_sem=lp_send.at[k],
            recv_sem=lp_recv.at[k],
            device_id={"proto": lax.rem(me + k, groups)},
            device_id_type=MESH,
        )

    def lz_copy(k):
        return pltpu.make_async_remote_copy(
            src_ref=loss_sum,
            dst_ref=loss_z.at[z],
            send_sem=lz_send.at[k],
            recv_sem=lz_recv.at[k],
            device_id={"dp": lax.rem(z + k, dp_count)},
            device_id_type=MESH,
        )

    def loss_begin():
        mine = jnp.broadcast_to(jnp.sum(loss_acc[...], axis=0, keepdims=True), (8, 128))
        too_big = jnp.where(bound_top[...] * inv_scale > BOUND, 1.0, 0.0)
        loss_mine[...] = jnp.where(lax.broadcasted_iota(jnp.int32, (8, 128), 0) < 4, mine, too_big)
        loss_plane[me] = loss_mine[...]
        for k in range(1, groups):
            lp_copy(k).start()

    def loss_middle():
        for k in range(1, groups):
            lp_copy(k).wait()
        plane = loss_plane[0]
        for k in range(1, groups):
            plane = plane + loss_plane[k]
        loss_sum[...] = plane
        loss_z[z] = plane
        for k in range(1, dp_count):
            lz_copy(k).start()

    def loss_end():
        for k in range(1, dp_count):
            lz_copy(k).wait()
        whole = loss_z[0]
        for k in range(1, dp_count):
            whole = whole + loss_z[k]
        loss_out[...] = whole * (1.0 / (rows * groups))

    def events(at):
        @pl.when((at < parts * chunks) & (lax.rem(at, chunks) == 0))
        def _():
            for g in range(parts):

                @pl.when(at == g * chunks)
                def _():
                    tiles_in(g)

            g = at // chunks
            new_block(g)

            @pl.when((z == 0) | (z == last))
            def _():
                way = jnp.where(z == 0, 0, 1)
                if coded:
                    new_bound(way, g, jnp.int32(0))

                def first_hop(c, carry):
                    if coded:
                        encode(way, g, c, scores[g, pl.ds(rows_of(way, c * chunk), chunk), :])
                    part_copy(way, g, c, True).start()
                    return carry

                lax.fori_loop(0, chunks, first_hop, 0)

        @pl.when(at == ret_start)
        def _():
            loss_begin()

        @pl.when(at >= ret_start)
        def _():
            send_pieces((at - ret_start) // dz_chunks)

    def step(i, at):
        way = lax.rem(i, 2)
        s = at + i // 2
        pos = jnp.where(way == 0, z, last - z)
        turn = s - lag(pos, LAG_FIRST, LAG, LAG_LAST)

        @pl.when((turn >= 0) & (turn < parts * chunks) & (pos > 0))
        def _():
            g = turn // chunks
            c = lax.rem(turn, chunks)

            if coded:

                @pl.when(c == 0)
                def _():
                    new_bound(way, g, pos)

            at = pl.ds(rows_of(way, c * chunk), chunk)

            @pl.when(pos < last)
            def _():
                part_copy(way, g, c, False).wait_recv()
                value = decode(way, g, c) + scores[g, at, :]
                if coded:
                    encode(way, g, c, value)
                else:
                    partial[way, g, pl.ds(pl.multiple_of(c * chunk, chunk), chunk), :] = value
                part_copy(way, g, c, False).start()

            @pl.when(pos == last)
            def _():
                part_copy(way, g, c, False).wait_recv()
                scores[g, at, :] += decode(way, g, c)

            @pl.when((pos == last) & (g == parts - 1))
            def _():
                lax.fori_loop(0, chunk // SOFT, softmax_rows, rows_of(way, c * chunk))

        d = s - dz_start - lag(last - pos, DZ_FIRST, DZ_LAG, DZ_LAST)
        u = jnp.where(d < tail_start, d // ratio, d - tail_start + dz_chunks)
        now = (d >= 0) & (u < parts * dz_chunks)
        now = now & ((d >= tail_start) | (lax.rem(d + ratio, ratio) == ratio - 1))

        @pl.when(now & (pos < last))
        def _():
            dz_copy(way, u).wait_recv()

        @pl.when(now & (pos > 0) & ((pos < last) | (u < dz_chunks)))
        def _():
            dz_copy(way, u).start()

        @pl.when(now & (pos == last) & (u == dz_chunks - 1))
        def _():
            def rest(later, carry):
                dz_copy(way, later).start()
                return carry

            lax.fori_loop(dz_chunks, parts * dz_chunks, rest, 0)

        return at

    def stage(j, carry):
        at = j * dz_chunks
        events(at)
        lax.fori_loop(0, 2 * dz_chunks, step, at)
        return carry

    lax.fori_loop(0, ret_start // dz_chunks + parts - 1, stage, 0)
    events(jnp.int32(ret_start + (parts - 1) * dz_chunks))
    loss_middle()

    def save_grad(i):
        at = pl.ds(pl.multiple_of(i * block, block), block)
        return pltpu.make_async_copy(grad.at[at], grad_hbm.at[at], grad_sem.at[i])

    def grad_block(i, carry):
        at = pl.ds(pl.multiple_of(i * block, block), block)
        total = jnp.dot(dz[0, at, :], tiles[0], preferred_element_type=jnp.float32)
        for g in range(1, parts):
            total = total + jnp.dot(dz[g, at, :], tiles[g], preferred_element_type=jnp.float32)
        grad[at, :] = total.astype(grad.dtype)
        save_grad(i).start()
        return carry

    lax.fori_loop(0, rows // block, grad_block, 0)

    loss_end()

    def drain_parts(i, carry):
        way = lax.rem(i, 2)
        turn = i // 2

        @pl.when(jnp.where(way == 0, z, last - z) < last)
        def _():
            part_copy(way, turn // chunks, lax.rem(turn, chunks), False).wait_send()

        return carry

    lax.fori_loop(0, 2 * parts * chunks, drain_parts, 0)

    def drain_dz(i, carry):
        way = lax.rem(i, 2)

        @pl.when(jnp.where(way == 0, z, last - z) > 0)
        def _():
            dz_copy(way, i // 2).wait_send()

        return carry

    lax.fori_loop(0, 2 * parts * dz_chunks, drain_dz, 0)
    if coded:

        def drain_bounds(i, carry):
            way = lax.rem(i, 2)

            @pl.when(jnp.where(way == 0, z, last - z) < last)
            def _():
                bound_copy(way, i // 2).wait_send()

            return carry

        lax.fori_loop(0, 2 * parts, drain_bounds, 0)
    for g in range(parts):
        for k in range(1, groups):
            tile_copy(g, k).wait_send()
    for i in range(rows // block):
        save_grad(i).wait()

    def drain_ret(q, carry):
        own_ret(q).wait()
        for k in range(1, groups):
            ret_copy(q, k).wait()
        return carry

    lax.fori_loop(0, parts, drain_ret, 0)


def run_main(coded, lists, labels, embeddings, table):
    block_rows, width = embeddings.shape
    list_len = lists.shape[1]
    tiles_here = table.shape[0] // TILE
    groups = lax.axis_size("proto")
    dp_count = lax.axis_size("dp")
    slots = groups * CAP
    cols = list_len * TILE // PARTS
    piece_rows = TILE // PARTS
    half = block_rows // 2
    chunks = half // CHUNK[coded]
    dz_chunks = half // DZ_CHUNK
    bf16, f32, i32 = jnp.bfloat16, jnp.float32, jnp.int32
    dma = pltpu.SemaphoreType.DMA
    vmem = pl.BlockSpec(memory_space=pltpu.VMEM)
    smem = pl.BlockSpec(memory_space=pltpu.SMEM)
    hbm = pl.BlockSpec(memory_space=pltpu.HBM)
    wire = (2, PARTS, half, cols)
    small = (2, PARTS, 8, 128)
    return pl.pallas_call(
        functools.partial(main_kernel, coded, groups, dp_count, tiles_here),
        out_shape=(
            jax.ShapeDtypeStruct((block_rows, width), bf16),
            jax.ShapeDtypeStruct((slots, TILE, width), bf16),
            jax.ShapeDtypeStruct((8, 128), f32),
            jax.ShapeDtypeStruct((8, 128), i32),
        ),
        in_specs=[smem, vmem, hbm, hbm],
        out_specs=(hbm, hbm, vmem, vmem),
        scratch_shapes=[
            pltpu.VMEM((tiles_here, TILE, width), bf16),
            pltpu.VMEM((block_rows, width), bf16),
            pltpu.VMEM((PARTS, slots, piece_rows, width), bf16),
            pltpu.VMEM((PARTS, cols, width), bf16),
            pltpu.VMEM((PARTS, block_rows, cols), f32),
            pltpu.VMEM(wire, jnp.int16 if coded else f32),
            pltpu.VMEM(wire if coded else (2, PARTS, 16, cols), jnp.int16),
            pltpu.VMEM(small, f32),
            pltpu.VMEM(small, f32),
            pltpu.VMEM(small, f32),
            pltpu.VMEM((8, 128), f32),
            pltpu.VMEM((block_rows, 128), i32),
            pltpu.VMEM((PARTS, block_rows, cols), bf16),
            pltpu.VMEM((list_len, piece_rows, width), bf16),
            pltpu.VMEM((PARTS, slots, piece_rows, width), bf16),
            pltpu.VMEM((block_rows, width), bf16),
            pltpu.VMEM((SOFT, 128), f32),
            pltpu.VMEM((8, 128), f32),
            pltpu.VMEM((groups, 8, 128), f32),
            pltpu.VMEM((8, 128), f32),
            pltpu.VMEM((dp_count, 8, 128), f32),
            pltpu.SMEM((slots,), i32),
            pltpu.SMEM((list_len,), i32),
            pltpu.SMEM((slots,), i32),
            dma,
            dma,
            dma((block_rows // 256,)),
            dma((PARTS, groups)),
            dma((PARTS, groups)),
            dma((2, PARTS, chunks)),
            dma((2, PARTS, chunks)),
            dma((2, PARTS)),
            dma((2, PARTS)),
            dma((2, PARTS * dz_chunks)),
            dma((2, PARTS * dz_chunks)),
            dma((PARTS, groups)),
            dma((PARTS, groups)),
            dma((PARTS,)),
            dma((groups,)),
            dma((groups,)),
            dma((dp_count,)),
            dma((dp_count,)),
        ]
        + [pltpu.VMEM((slots, piece_rows, width), bf16)] * PARTS,
        compiler_params=pltpu.CompilerParams(
            collective_id=int(coded), has_side_effects=True, vmem_limit_bytes=VMEM_LIMIT
        ),
    )(lists, labels.reshape(block_rows // 128, 128), embeddings, table.reshape(tiles_here, TILE, width))


def fused_body(embeddings, table, tile_lists, labels):
    tiles_here = table.shape[0] // TILE
    inputs = (tile_lists, labels, embeddings, table)

    def finish(grad_emb, returned, loss, plan):
        return place_tiles(plan, returned, grad_emb, loss, tiles_here)

    if GUARD == 0:
        grad_table, grad_emb, loss = finish(*run_main(True, *inputs))
    else:
        coded = run_main(True, *inputs)
        grad_table, grad_emb, loss = lax.cond(
            coded[2][7, 0] > 0.0,
            lambda coded, inputs: finish(*run_main(False, *inputs)),
            lambda coded, inputs: finish(*coded),
            coded,
            inputs,
        )
    return (loss.reshape(()), grad_emb, grad_table.reshape(table.shape))


def any_body(embeddings, table, tile_lists, labels):
    block_rows, width = embeddings.shape
    cols = tile_lists.shape[1] * TILE
    need = block_rows * cols * (4 + 4 + 2 + 2) + 2 * table.shape[0] * width * 2
    if need + 8 * 2**20 <= VMEM_LIMIT and block_rows % 1024 == 0:
        return fused_body(embeddings, table, tile_lists, labels)
    return body(embeddings, table, tile_lists, labels)


def solution(mesh):
    placed = (P("proto", "dp"), P("proto", "dp"), P(), P("proto"))
    return jax.shard_map(
        any_body,
        mesh=mesh,
        in_specs=placed,
        out_specs=(P(), P("proto", "dp"), P("proto", "dp")),
        check_vma=False,
    )
```
